32 devices in a mesh: ta: 4 (over z), ha: 2 (over y), wa: 4 (over x, core).
Axes of the slice: x: 2, y: 2, z: 4, core: 2. Of those that a mesh axis runs over, the one named last changes fastest.
Arguments:
- stream: bfloat16 [4, 2, 384, 1536], P('ta', 'ha'), may hold values from -40 to 40
- queries: bfloat16 [4, 2, 384, 1536], P('ta', 'ha', None, 'wa'), may hold values from -6 to 6
- key_heads: bfloat16 [4, 2, 384, 1536], P('ta', 'ha', None, 'wa'), may hold values from -6 to 6
- value_heads: bfloat16 [4, 2, 384, 1536], P('ta', 'ha', None, 'wa'), may hold values from -6 to 6
- out_weight: bfloat16 [1536, 1536], P('wa'), may hold values from -0.15625 to 0.15625
- norm_gain: float32 [1536], replicated, may hold values from 0.25 to 1.75
- up_weight: bfloat16 [1536, 6144], P(('ta', 'ha'), 'wa'), may hold values from -0.15625 to 0.15625
- down_weight: bfloat16 [6144, 1536], P('wa', ('ta', 'ha')), may hold values from -0.078125 to 0.078125
- tile_route: int32 [4, 2, 1], P('ta', 'ha'), may hold values 0 or 1
- cotangent: bfloat16 [4, 2, 384, 1536], P('ta', 'ha'), may hold values from -6 to 6
Outputs:
- stream_grad: bfloat16 [4, 2, 384, 1536], P('ta', 'ha')
- query_grad: bfloat16 [4, 2, 384, 1536], P('ta', 'ha', None, 'wa')
- key_grad: bfloat16 [4, 2, 384, 1536], P('ta', 'ha', None, 'wa')
- value_grad: bfloat16 [4, 2, 384, 1536], P('ta', 'ha', None, 'wa')
- out_weight_grad: float32 [1536, 1536], P('wa', ('ta', 'ha'))
The draws below stay inside these ranges and needn't reach their ends.
All inputs are finite; a program needn't handle non-finite values. No bound on the sum of `tile_route` on one device may be relied on, other than what follows from the above.
Results may differ from the reference program's by a relative error of at most 0.014.
Values may be sent and summed in bfloat16 or wider, within the bound.
A program may use at most 128 MiB of HBM per device.

```python
import math
import jax
import jax.numpy as jnp
from jax import lax

D = 1536
HEADS = 12
HS = 128
FF = 6144
WT = 1
TILE = 384
ROWS = 384
TILES_T = 4
TILES_H = 2


def query_key_pair(key):
    full_shape = (TILES_T, TILES_H, ROWS, HEADS * HS)
    query_base = jnp.clip(jax.random.normal(jax.random.fold_in(key, 101), full_shape, jnp.float32), -6.0, 6.0)
    key_base = jnp.clip(jax.random.normal(jax.random.fold_in(key, 102), full_shape, jnp.float32), -6.0, 6.0)
    return (query_base, key_base)


def draw_queries(key, part):
    return query_key_pair(key)[0].astype(jnp.bfloat16)


def draw_key_heads(key, part):
    return query_key_pair(key)[1].astype(jnp.bfloat16)


def draw_stream(key, part):
    full_shape = (TILES_T, TILES_H, ROWS, D)
    values = jnp.clip(jax.random.normal(jax.random.fold_in(key, 201), full_shape, jnp.float32), -4.0, 4.0)
    row_scale = jnp.exp(jax.random.uniform(jax.random.fold_in(key, 202), (TILES_T, TILES_H, ROWS, 1), jnp.float32, math.log(0.3), math.log(3.0)))
    column_scale = jnp.exp(jax.random.uniform(jax.random.fold_in(key, 203), (1, 1, 1, D), jnp.float32, math.log(0.3), math.log(3.0)))
    values = values * row_scale * column_scale
    return values.astype(jnp.bfloat16)


def with_ends(entries, stream_key, low, top_value):
    spot = [jax.random.randint(jax.random.fold_in(stream_key, axis), (), 0, length) for axis, length in enumerate(entries.shape)]
    main_axis = entries.shape.index(max(entries.shape))
    next_to = spot[:main_axis] + [(spot[main_axis] + 1) % entries.shape[main_axis]] + spot[main_axis + 1:]
    return entries.at[tuple(spot)].set(low).at[tuple(next_to)].set(top_value)


def steps_of(rng, dims, split, smallest, top_value):
    level, own = 1.0, jax.random.fold_in(rng, 6)
    for dim, blocks in split:
        draws = jnp.exp(jax.random.uniform(jax.random.fold_in(own, dim), (blocks,), jnp.float32, smallest / len(split), top_value / len(split)))
        level = level * jnp.repeat(draws, dims[dim] // blocks).reshape([-1 if axis == dim else 1 for axis in range(len(dims))])
    return level


def normal_values(own_key, shape, width, limit, pieces=(), kind=jnp.bfloat16):
    loudness = steps_of(own_key, shape, pieces, -0.22, 0.18) if pieces else 1.0
    entries = jax.random.normal(own_key, shape, jnp.float32) * width * loudness
    return jnp.minimum(jnp.maximum(entries, -limit), limit).astype(kind)


def setup_inputs(seed: int = 0) -> dict:
    keys = jax.random.split(jax.random.key(seed), 11)
    return {
        "stream": draw_stream(jax.random.fold_in(keys[10], 71), 0),
        "queries": draw_queries(jax.random.fold_in(keys[10], 71), 0),
        "key_heads": draw_key_heads(jax.random.fold_in(keys[10], 71), 0),
        "value_heads": normal_values(keys[3], (TILES_T, TILES_H, ROWS, HEADS * HS), 1.0, 6.0, ((0, 4), (1, 2), (3, 4))),
        "out_weight": normal_values(keys[4], (HEADS * HS, D), (HEADS * HS) ** -0.5, 0.15625, ((0, 4),)),
        "norm_gain": jnp.clip(1.0 + 0.15 * jax.random.normal(keys[5], (D,), jnp.float32), 0.25, 1.75),
        "up_weight": normal_values(keys[6], (D, FF), D ** -0.5, 0.15625, ((0, 8), (1, 4))),
        "down_weight": normal_values(keys[7], (FF, D), FF ** -0.5, 0.078125, ((0, 4), (1, 8))),
        "tile_route": with_ends((jax.random.randint(keys[8], (TILES_T, TILES_H, WT), 0, 2) < 1).astype(jnp.int32), jax.random.fold_in(keys[8], 1), 0, 1),
        "cotangent": normal_values(keys[9], (TILES_T, TILES_H, ROWS, D), 1.0, 6.0, ((0, 4), (1, 2))),
    }


EPSILON = 1e-06
TANH_SCALE = 0.7978845608028654
CUBIC_COEF = 0.044715
NEG_FILL = -1e+30

def gelu_slope(pre_act):
    tanh_arg = TANH_SCALE * (pre_act + CUBIC_COEF * pre_act * pre_act * pre_act)
    tanh_val = jnp.tanh(tanh_arg)
    return 0.5 * (1.0 + tanh_val) + 0.5 * pre_act * (1.0 - tanh_val * tanh_val) * TANH_SCALE * (1.0 + 3.0 * CUBIC_COEF * pre_act * pre_act)

def rounded(values):
    return lax.optimization_barrier(values.astype(jnp.bfloat16)).astype(jnp.float32)

def window_probs(query_tile, key_block, key_marks, score_scale):
    scores = jnp.einsum('qhd,khd->hqk', query_tile.astype(jnp.float32), key_block.astype(jnp.float32)) * score_scale
    scores = jnp.where(key_marks[None, None, :] > 0.5, scores, NEG_FILL)
    row_max = lax.optimization_barrier(jnp.max(scores, axis=2))
    weights = jnp.exp(scores - row_max[:, :, None])
    row_total = lax.optimization_barrier(jnp.sum(weights, axis=2))
    return weights / row_total[:, :, None]

def layer_norm(residual):
    mean_val = lax.optimization_barrier(jnp.mean(residual, axis=1, keepdims=True))
    centered = residual - mean_val
    variance = lax.optimization_barrier(jnp.mean(centered * centered, axis=1, keepdims=True))
    inv_std = lax.rsqrt(variance + EPSILON)
    return (centered * inv_std, inv_std)

def norm_backward(norm_grad, norm_gain, normed, inv_std):
    scaled = norm_grad * norm_gain
    return (scaled - lax.optimization_barrier(jnp.mean(scaled, axis=1, keepdims=True)) - normed * lax.optimization_barrier(jnp.mean(scaled * normed, axis=1, keepdims=True))) * inv_std

def reference(stream, queries, key_heads, value_heads, out_weight, norm_gain, up_weight, down_weight, tile_route, cotangent):
    tiles_t, tiles_h, row_count, model_width = stream.shape
    channels = queries.shape[3]
    per_row = row_count // TILE
    tile_total = tiles_t * tiles_h * per_row
    token_total = tiles_t * tiles_h * row_count
    score_scale = 1.0 / math.sqrt(HS)
    anchor = jnp.zeros((), jnp.int32)
    pad_spec = ((1, 1), (1, 1), (0, 0), (0, 0))
    key_pad = jnp.pad(key_heads, pad_spec)
    value_pad = jnp.pad(value_heads, pad_spec)
    mark_pad = jnp.pad(tile_route.astype(jnp.float32), ((1, 1), (1, 1), (0, 0)))
    block_size = (3, 3, TILE, channels)

    def window(flat_index):
        flat_index = flat_index.astype(jnp.int32)
        along_t = (flat_index // (tiles_h * per_row)).astype(jnp.int32)
        along_h = (flat_index // per_row % tiles_h).astype(jnp.int32)
        along_w = (flat_index % per_row).astype(jnp.int32)
        row_start = (along_w * TILE).astype(jnp.int32)
        key_start = (along_t, along_h, row_start, anchor)
        own_start = (along_t, along_h, row_start, anchor)
        key_block = lax.dynamic_slice(key_pad, key_start, block_size).reshape(9 * TILE, HEADS, HS)
        value_block = lax.dynamic_slice(value_pad, key_start, block_size).reshape(9 * TILE, HEADS, HS)
        mark_block = lax.dynamic_slice(mark_pad, (along_t, along_h, along_w), (3, 3, 1)).reshape(9)
        key_marks = jnp.repeat(mark_block, TILE)
        query_tile = lax.dynamic_slice(queries, own_start, (1, 1, TILE, channels)).reshape(TILE, HEADS, HS)
        own_mark = mark_pad[along_t + 1, along_h + 1, along_w]
        return (query_tile, key_block, value_block, key_marks, own_mark, key_start, own_start)

    def forward_tile(flat_index):
        query_tile, key_block, value_block, key_marks, own_mark, key_start, own_start = window(flat_index)
        weights = window_probs(query_tile, key_block, key_marks, score_scale)
        mixture = jnp.einsum('hqk,khd->qhd', rounded(weights), value_block.astype(jnp.float32))
        return (mixture * own_mark).astype(jnp.bfloat16).reshape(TILE, channels)
    attention = lax.map(forward_tile, jnp.arange(tile_total, dtype=jnp.int32)).reshape(token_total, channels)
    residual = stream.reshape(token_total, model_width).astype(jnp.float32) + jnp.dot(attention, out_weight, preferred_element_type=jnp.float32)
    normed, inv_std = layer_norm(residual)
    hidden_in = (normed * norm_gain).astype(jnp.bfloat16)
    flat_cot = cotangent.reshape(token_total, model_width)

    def mlp_block(block_index):
        row_start = block_index.astype(jnp.int32) * TILE
        hidden_rows = lax.dynamic_slice_in_dim(hidden_in, row_start, TILE, 0)
        cot_rows = lax.dynamic_slice_in_dim(flat_cot, row_start, TILE, 0)
        pre_act = jnp.dot(hidden_rows, up_weight, preferred_element_type=jnp.float32)
        act_grad = jnp.dot(cot_rows, down_weight.T, preferred_element_type=jnp.float32)
        pre_grad = (act_grad * gelu_slope(pre_act)).astype(jnp.bfloat16)
        return jnp.dot(pre_grad, up_weight.T, preferred_element_type=jnp.float32)
    norm_grad = lax.map(mlp_block, jnp.arange(token_total // TILE, dtype=jnp.int32)).reshape(token_total, model_width)
    residual_grad = flat_cot.astype(jnp.float32) + norm_backward(norm_grad, norm_gain, normed, inv_std)
    stream_grad = residual_grad.astype(jnp.bfloat16)
    out_weight_grad = jnp.dot(attention.T, stream_grad, preferred_element_type=jnp.float32)
    attn_grad = jnp.dot(stream_grad, out_weight.T, preferred_element_type=jnp.float32).astype(jnp.bfloat16)
    grad_grid = attn_grad.reshape(tiles_t, tiles_h, row_count, channels)

    def backward_tile(flat_index, carried):
        key_acc, value_acc, query_grad = carried
        query_tile, key_block, value_block, key_marks, own_mark, key_start, own_start = window(flat_index)
        grad_tile = lax.dynamic_slice(grad_grid, own_start, (1, 1, TILE, channels)).reshape(TILE, HEADS, HS).astype(jnp.float32) * own_mark
        weights = window_probs(query_tile, key_block, key_marks, score_scale)
        grad_probs = jnp.einsum('qhd,khd->hqk', grad_tile, value_block.astype(jnp.float32))
        row_delta = lax.optimization_barrier(jnp.sum(weights * grad_probs, axis=2))
        grad_scores = rounded(weights * (grad_probs - row_delta[:, :, None]) * score_scale)
        query_part = jnp.einsum('hqk,khd->qhd', grad_scores, key_block.astype(jnp.float32)).astype(jnp.bfloat16).reshape(1, 1, TILE, channels)
        value_part = rounded(jnp.einsum('hqk,qhd->khd', rounded(weights), grad_tile)).reshape(block_size)
        key_part = rounded(jnp.einsum('hqk,qhd->khd', grad_scores, query_tile.astype(jnp.float32))).reshape(block_size)
        key_acc = lax.dynamic_update_slice(key_acc, lax.dynamic_slice(key_acc, key_start, block_size) + key_part, key_start)
        value_acc = lax.dynamic_update_slice(value_acc, lax.dynamic_slice(value_acc, key_start, block_size) + value_part, key_start)
        query_grad = lax.dynamic_update_slice(query_grad, query_part, own_start)
        return (key_acc, value_acc, query_grad)
    acc_shape = (tiles_t + 2, tiles_h + 2, row_count, channels)
    start_carry = (jnp.zeros(acc_shape, jnp.float32), jnp.zeros(acc_shape, jnp.float32), jnp.zeros(queries.shape, jnp.bfloat16))
    key_acc, value_acc, query_grad = lax.fori_loop(0, tile_total, backward_tile, start_carry)
    key_grad = key_acc[1:-1, 1:-1].astype(jnp.bfloat16)
    value_grad = value_acc[1:-1, 1:-1].astype(jnp.bfloat16)
    return (stream_grad.reshape(stream.shape), query_grad, key_grad, value_grad, out_weight_grad)
```

```python
import functools
import math

import jax
import jax.numpy as jnp
from jax import lax
from jax.experimental import pallas as pl
from jax.experimental.pallas import tpu as pltpu
from jax.sharding import PartitionSpec as P

HS = 128
TILE = 384


EPSILON = 1e-06
TANH_SCALE = 0.7978845608028654
CUBIC_COEF = 0.044715
NEG_FILL = -1e30


def extended(cells, sides, width):
    for axis, dim in sides:
        count = lax.axis_size(axis)
        ends = count - 1
        head = lax.slice_in_dim(cells, 0, width, axis=dim)
        tail = lax.slice_in_dim(cells, cells.shape[dim] - width, cells.shape[dim], axis=dim)
        cells = jnp.concatenate(
            [
                lax.ppermute(tail, axis, [(i, (i + 1) % count) for i in range(ends)]),
                cells,
                lax.ppermute(head, axis, [((i + 1) % count, i) for i in range(ends)]),
            ],
            axis=dim,
        )
    return cells


def from_behind(array, axis, by):
    devices = lax.axis_size(axis)
    pairs = [(i, i + by) for i in range(devices) if 0 <= i + by < devices]
    return lax.ppermute(array, axis, pairs)


def gelu_slope(pre_act):
    tanh_arg = TANH_SCALE * (pre_act + CUBIC_COEF * pre_act * pre_act * pre_act)
    tanh_val = jnp.tanh(tanh_arg)
    return 0.5 * (1.0 + tanh_val) + 0.5 * pre_act * (1.0 - tanh_val * tanh_val) * TANH_SCALE * (
        1.0 + 3.0 * CUBIC_COEF * pre_act * pre_act
    )


def head_probs(query_rows, key_rows, key_marks, score_scale):
    scores = (
        jnp.einsum("qd,kd->qk", query_rows, key_rows, preferred_element_type=jnp.float32)
        * score_scale
    )
    scores = jnp.where(key_marks[None, :] > 0.5, scores, NEG_FILL)
    row_max = jnp.max(scores, axis=1)
    weights = jnp.exp(scores - row_max[:, None])
    row_total = jnp.sum(weights, axis=1)
    return (weights / row_total[:, None], row_max, row_total)


def layer_norm(residual):
    mean_val = jnp.mean(residual, axis=1, keepdims=True)
    centered = residual - mean_val
    variance = jnp.mean(centered * centered, axis=1, keepdims=True)
    inv_std = lax.rsqrt(variance + EPSILON)
    return (centered * inv_std, inv_std)


def norm_backward(norm_grad, norm_gain, normed, inv_std):
    scaled = norm_grad * norm_gain
    return (
        scaled
        - jnp.mean(scaled, axis=1, keepdims=True)
        - normed * jnp.mean(scaled * normed, axis=1, keepdims=True)
    ) * inv_std


def shards(
    stream,
    queries,
    key_heads,
    value_heads,
    out_weight,
    norm_gain,
    up_weight,
    down_weight,
    tile_route,
    cotangent,
):
    row_count = stream.shape[2]
    model_width = stream.shape[3]
    channels = queries.shape[3]
    heads_here = channels // HS
    tile_count = row_count // TILE
    score_scale = 1.0 / math.sqrt(HS)
    tile_ids = jnp.arange(tile_count, dtype=jnp.int32)
    tile_marks = tile_route.astype(jnp.bfloat16)
    faces_key, faces_value, faces_marks = (
        extended(key_heads, (("ta", 0), ("ha", 1)), 1),
        extended(value_heads, (("ta", 0), ("ha", 1)), 1),
        extended(tile_marks, (("ta", 0), ("ha", 1)), 1),
    )

    def window():
        key_block = faces_key.reshape(9 * TILE, heads_here, HS)
        value_block = faces_value.reshape(9 * TILE, heads_here, HS)
        mark_block = faces_marks.reshape(9).astype(jnp.float32)
        key_marks = jnp.repeat(mark_block, TILE)
        query_tile = queries.reshape(TILE, heads_here, HS)
        return (
            query_tile.transpose(1, 0, 2),
            key_block.transpose(1, 0, 2),
            value_block.transpose(1, 0, 2),
            key_marks,
        )

    def forward_tile(tile_index):
        own_mark = tile_marks[0, 0, tile_index]
        query_tile, key_block, value_block, key_marks = window()

        def per_head(operands):
            query_rows, key_rows, value_rows = operands
            weights, row_max, row_total = head_probs(query_rows, key_rows, key_marks, score_scale)
            mixture = jnp.dot(
                weights.astype(jnp.bfloat16), value_rows, preferred_element_type=jnp.float32
            )
            return (mixture, row_max, row_total)

        mixture, row_max, row_total = lax.map(per_head, (query_tile, key_block, value_block))
        scaled = (mixture * own_mark.astype(jnp.float32)).astype(jnp.bfloat16)
        return (scaled.transpose(1, 0, 2).reshape(TILE, channels), row_max, row_total)

    attn_tiles, max_tiles, total_tiles = lax.map(forward_tile, tile_ids)
    attention = attn_tiles.reshape(row_count, channels)
    attn_part = jnp.dot(attention, out_weight, preferred_element_type=jnp.float32)
    head_share = lax.psum_scatter(attn_part, "wa", scatter_dimension=0, tiled=True)
    share_rows = head_share.shape[0]
    share_start = lax.axis_index("wa") * share_rows
    flat_stream = stream.reshape(row_count, model_width)
    flat_cot = cotangent.reshape(row_count, model_width)
    residual = (
        lax.dynamic_slice_in_dim(flat_stream, share_start, share_rows, 0).astype(jnp.float32)
        + head_share
    )
    normed, inv_std = layer_norm(residual)
    hidden_share = (normed * norm_gain).astype(jnp.bfloat16)
    hidden_in = lax.all_gather(hidden_share, "wa", axis=0, tiled=True)
    up_full, down_full = (
        lax.all_gather(up_weight, ("ta", "ha"), axis=0, tiled=True),
        lax.all_gather(down_weight, ("ta", "ha"), axis=1, tiled=True),
    )
    pre_act = jnp.dot(hidden_in, up_full, preferred_element_type=jnp.float32)
    act_grad = jnp.einsum("td,fd->tf", flat_cot, down_full, preferred_element_type=jnp.float32)
    pre_grad = (act_grad * gelu_slope(pre_act)).astype(jnp.bfloat16)
    norm_part = jnp.einsum("tf,df->td", pre_grad, up_full, preferred_element_type=jnp.float32)
    norm_share = lax.psum_scatter(norm_part, "wa", scatter_dimension=0, tiled=True)
    cot_share = lax.dynamic_slice_in_dim(flat_cot, share_start, share_rows, 0).astype(jnp.float32)
    grad_share = (cot_share + norm_backward(norm_share, norm_gain, normed, inv_std)).astype(
        jnp.bfloat16
    )
    stream_grad = lax.all_gather(grad_share, "wa", axis=0, tiled=True)
    weight_part = jnp.einsum(
        "tc,td->cd", attention, stream_grad, preferred_element_type=jnp.float32
    )
    out_weight_grad = lax.psum_scatter(weight_part, ("ta", "ha"), scatter_dimension=1, tiled=True)
    attn_grad = jnp.einsum(
        "td,cd->tc", stream_grad, out_weight, preferred_element_type=jnp.float32
    ).astype(jnp.bfloat16)
    row_marks = jnp.repeat(tile_marks.reshape(tile_count), TILE)
    masked_grad = attn_grad * row_marks[:, None]

    def own_side():
        query_tile, key_block, value_block, key_marks = window()
        grad_tile = masked_grad.reshape(TILE, heads_here, HS).transpose(1, 0, 2)

        def head_back(operands):
            query_rows, key_rows, value_rows, grad_rows = operands
            weights = head_probs(query_rows, key_rows, key_marks, score_scale)[0]
            grad_probs = jnp.einsum(
                "qd,kd->qk", grad_rows, value_rows, preferred_element_type=jnp.float32
            )
            row_delta = jnp.sum(weights * grad_probs, axis=1)
            grad_scores = (weights * (grad_probs - row_delta[:, None]) * score_scale).astype(
                jnp.bfloat16
            )
            query_part = jnp.dot(grad_scores, key_rows, preferred_element_type=jnp.float32).astype(
                jnp.bfloat16
            )
            value_part = jnp.einsum(
                "qk,qd->kd",
                weights.astype(jnp.bfloat16),
                grad_rows,
                preferred_element_type=jnp.float32,
            ).astype(jnp.bfloat16)
            key_part = jnp.einsum(
                "qk,qd->kd", grad_scores, query_rows, preferred_element_type=jnp.float32
            ).astype(jnp.bfloat16)
            return (query_part, row_delta, key_part, value_part)

        results = lax.map(head_back, (query_tile, key_block, value_block, grad_tile))
        query_part = results[0].transpose(1, 0, 2).reshape(TILE, channels)
        key_part = results[2].transpose(1, 0, 2).reshape(3, 3, TILE, channels)
        value_part = results[3].transpose(1, 0, 2).reshape(3, 3, TILE, channels)
        return (query_part, results[1], key_part, value_part)

    def guarded_own():
        blank_parts = (
            jnp.zeros((TILE, channels), jnp.bfloat16),
            jnp.zeros((heads_here, TILE), jnp.float32),
        )
        blank_parts = blank_parts + (
            jnp.zeros((3, 3, TILE, channels), jnp.bfloat16),
            jnp.zeros((3, 3, TILE, channels), jnp.bfloat16),
        )
        return own_side()

    def place_tile(carried, tile_index):
        query_part, row_delta, key_part, value_part = guarded_own()
        return ((key_part, value_part), query_part)

    empty_slots = jnp.zeros((3, 3, row_count, channels), jnp.bfloat16)
    (slots_key, slots_value), query_parts = lax.scan(
        place_tile, (empty_slots, empty_slots), tile_ids
    )
    middle_key = slots_key[1].astype(jnp.float32)
    middle_value = slots_value[1].astype(jnp.float32)
    for by_step, source in ((-1, 0), (1, 2)):
        moved_key, moved_value = from_behind(
            (slots_key[source], slots_value[source]), "ta", by_step
        )
        middle_key = middle_key + moved_key.astype(jnp.float32)
        middle_value = middle_value + moved_value.astype(jnp.float32)
    final_key = middle_key[1]
    final_value = middle_value[1]
    for by_step, source in ((-1, 0), (1, 2)):
        moved_key, moved_value = (
            from_behind(middle_key[source].astype(jnp.bfloat16), "ha", by_step).astype(jnp.float32),
            from_behind(middle_value[source].astype(jnp.bfloat16), "ha", by_step).astype(
                jnp.float32
            ),
        )
        final_key = final_key + moved_key
        final_value = final_value + moved_value
    key_grad = final_key.astype(jnp.bfloat16).reshape(1, 1, row_count, channels)
    value_grad = final_value.astype(jnp.bfloat16).reshape(1, 1, row_count, channels)
    query_grad = query_parts.reshape(1, 1, row_count, channels)
    return (
        stream_grad.reshape(1, 1, row_count, model_width),
        query_grad,
        key_grad,
        value_grad,
        out_weight_grad,
    )


MESH = pl.DeviceIdType.MESH
WINDOW = 9
CENTRE = 4


def step_kernel(
    n_t, n_h, n_w, kvm, q, stream, cot, ow, gain, upw, dnw,
    sg, qg, kg, vg, wg,
    kv, up, dn, score, top, total, probs, mix, att, apart, arecv, hid, normed, inv,
    act, pgrad, npart, nrecv, gmask, wsend, wrecv, psend, precv,
    halo_s, halo_r, wt_s, wt_r, r1_s, r1_r, a1_s, a1_r, r2_s, r2_r, a2_s, a2_r,
    wg_s, wg_r, pt_s, pt_r,
):
    f32, bf16 = jnp.float32, jnp.bfloat16
    t, h, w = lax.axis_index("ta"), lax.axis_index("ha"), lax.axis_index("wa")
    n = n_t * n_h
    g = t * n_h + h
    rows, width = stream.shape
    channels = q.shape[1]
    heads = channels // HS
    slab = upw.shape[0]
    share = rows // n_w
    hidden = upw.shape[1]
    score_scale = 1.0 / math.sqrt(HS)
    pending = []

    def at_group(tt, hh):
        return {"ta": tt, "ha": hh}

    def at_wa(ww):
        return {"wa": ww}

    def group_peer(k):
        idx = lax.rem(g + k, n)
        return idx, at_group(idx // n_h, lax.rem(idx, n_h))

    def send(src, dst, s_sem, r_sem, dev, cond=None):
        copy = pltpu.make_async_remote_copy(
            src_ref=src, dst_ref=dst, send_sem=s_sem, recv_sem=r_sem,
            device_id=dev, device_id_type=MESH,
        )
        if cond is None:
            copy.start()
        else:
            pl.when(cond)(copy.start)
        pending.append((copy, cond))

    def arrived(dst, s_sem, r_sem, dev, cond=None):
        copy = pltpu.make_async_remote_copy(
            src_ref=dst, dst_ref=dst, send_sem=s_sem, recv_sem=r_sem,
            device_id=dev, device_id_type=MESH,
        )
        if cond is None:
            copy.wait_recv()
        else:
            pl.when(cond)(copy.wait_recv)

    def inside(tt, hh):
        return (tt >= 0) & (tt < n_t) & (hh >= 0) & (hh < n_h)

    def place(slot):
        return t + slot // 3 - 1, h + slot % 3 - 1

    def w_rows(ww):
        return pl.ds(pl.multiple_of(ww * share, share), share)

    def slab_rows(idx):
        return pl.ds(pl.multiple_of(idx * slab, slab), slab)

    barrier = pltpu.get_barrier_semaphore()
    for k in range(1, n):
        pl.semaphore_signal(barrier, inc=1, device_id=group_peer(k)[1], device_id_type=MESH)
    for k in range(1, n_w):
        pl.semaphore_signal(barrier, inc=1, device_id=at_wa(lax.rem(w + k, n_w)), device_id_type=MESH)
    pl.semaphore_wait(barrier, n - 1 + n_w - 1)

    for slot in (1, 7, 3, 5, 0, 2, 6, 8):
        tt, hh = place(slot)
        send(kvm, kv.at[8 - slot], halo_s.at[slot], halo_r.at[8 - slot], at_group(tt, hh), inside(tt, hh))

    weights = (dn, up)

    def hop(which, src_ref, idx, way):
        tt, hh = ((t + 1, h), (t - 1, h), (t, h + 1), (t, h - 1))[way]
        return (
            src_ref, weights[which].at[slab_rows(idx)], wt_s.at[which, way, idx],
            wt_r.at[which, idx], at_group(tt, hh),
        ), inside(tt, hh)

    def forward(which, src_ref, idx, ways, cond=None):
        for way in ways:
            args, here = hop(which, src_ref, idx, way)
            send(*args, here if cond is None else here & cond)

    forward(0, dnw, g, (2, 3, 0, 1))
    forward(1, upw, g, (2, 3, 0, 1))

    def relay(which, d):
        for sign, way in ((1, 0), (-1, 1)):
            tt = t - sign * d
            cond = inside(tt, h)
            idx = jnp.clip(tt, 0, n_t - 1) * n_h + h
            block = weights[which].at[slab_rows(idx)]
            arrived(block, wt_s.at[which, way, idx], wt_r.at[which, idx], at_group(t, h), cond)
            forward(which, block, idx, (2, 3, way), cond)

    def finish(which):
        for e in range(1, n_h):
            for sign, way in ((1, 2), (-1, 3)):
                hh = h - sign * e
                for d in range(-(n_t - 1), n_t):
                    tt = t + d
                    cond = inside(tt, hh)
                    idx = jnp.clip(tt, 0, n_t - 1) * n_h + jnp.clip(hh, 0, n_h - 1)
                    block = weights[which].at[slab_rows(idx)]
                    arrived(block, wt_s.at[which, way, idx], wt_r.at[which, idx], at_group(t, h), cond)
                    if e < n_h - 1:
                        forward(which, block, idx, (way,), cond)

    kv[CENTRE] = kvm[...]
    dn[slab_rows(g), :] = dnw[...]
    up[slab_rows(g), :] = upw[...]

    for slot in (1, 7, 3, 5, 0, 2, 6, 8):
        tt, hh = place(slot)
        arrived(kv.at[slot], halo_s.at[slot], halo_r.at[slot], at_group(t, h), inside(tt, hh))

    def each_tile(work):
        @pl.loop(0, WINDOW)
        def _(slot):
            tt, hh = place(slot)
            pl.when(inside(tt, hh))(lambda: work(slot))

    nt = (((1,), (1,)), ((), ()))
    tn = (((0,), (0,)), ((), ()))
    key_rows, value_rows = pl.ds(0, TILE), pl.ds(TILE, TILE)
    own_mark = kvm[pl.ds(2 * TILE, 1), :].astype(f32)

    def attend(e):
        cols = pl.ds(e * HS, HS)
        top[...] = jnp.full(top.shape, NEG_FILL, f32)
        total[...] = jnp.zeros(total.shape, f32)
        mix[:, cols] = jnp.zeros((rows, HS), f32)

        def raw(slot):
            s = lax.dot_general(q[:, cols], kv[slot, key_rows, cols], nt, preferred_element_type=f32)
            mark = kv[slot, pl.ds(2 * TILE, 1), :].astype(f32)
            s = jnp.where(mark > 0.5, s * score_scale, NEG_FILL)
            score[slot] = s
            top[...] = jnp.maximum(top[...], jnp.max(s, axis=1, keepdims=True))

        each_tile(raw)

        def expo(slot):
            p = jnp.exp(score[slot] - top[:, 0:1])
            score[slot] = p
            total[...] = total[...] + jnp.sum(p, axis=1, keepdims=True)

        each_tile(expo)
        total[...] = 1.0 / total[...]

        def blend(slot):
            p = (score[slot] * total[:, 0:1]).astype(bf16)
            probs[e, slot] = p
            mix[:, cols] = mix[:, cols] + jnp.dot(p, kv[slot, value_rows, cols], preferred_element_type=f32)

        each_tile(blend)

    for e in range(heads):
        attend(e)
        if e == heads - 2:
            relay(0, 1)
    att[...] = (mix[...] * own_mark).astype(bf16)
    step = 512

    def col_tiles(count, work):
        @pl.loop(0, count // step)
        def _(c):
            work(pl.ds(pl.multiple_of(c * step, step), step))

    def project(cols):
        apart[:, cols] = jnp.dot(att[...], ow[:, cols], preferred_element_type=f32).astype(bf16)

    col_tiles(width, project)
    for k in range(1, n_w):
        ww = lax.rem(w + k, n_w)
        send(apart.at[w_rows(ww)], arecv.at[k], r1_s.at[k], r1_r.at[k], at_wa(ww))
    relay(1, 1)
    resid = stream[w_rows(w), :].astype(f32) + apart[w_rows(w), :].astype(f32)
    for k in range(1, n_w):
        arrived(arecv.at[k], r1_s.at[k], r1_r.at[k], at_wa(w))
        resid = resid + arecv[k].astype(f32)
    centered = resid - jnp.mean(resid, axis=1, keepdims=True)
    istd = lax.rsqrt(jnp.mean(centered * centered, axis=1, keepdims=True) + EPSILON)
    inv[...] = jnp.broadcast_to(istd, inv.shape)
    normed[...] = centered * istd
    hid[w_rows(w), :] = (normed[...] * gain[...]).astype(bf16)
    for k in range(1, n_w):
        send(hid.at[w_rows(w)], hid.at[w_rows(w)], a1_s.at[k], a1_r.at[k], at_wa(lax.rem(w + k, n_w)))
    for d in range(2, n_t):
        relay(0, d)
        relay(1, d)
    finish(0)

    def act_tile(cols):
        act[:, cols] = jnp.dot(cot[...], dn[:, cols], preferred_element_type=f32)

    col_tiles(hidden, act_tile)
    for k in range(1, n_w):
        arrived(hid.at[w_rows(lax.rem(w + n_w - k, n_w))], a1_s.at[k], a1_r.at[k], at_wa(w))
    finish(1)

    def grad_tile(cols):
        pre = jnp.dot(hid[...], up[:, cols], preferred_element_type=f32)
        pgrad[:, cols] = (act[:, cols] * gelu_slope(pre)).astype(bf16)

    col_tiles(hidden, grad_tile)
    for c in range(width // step):
        cols = pl.ds(c * step, step)
        npart[:, cols] = lax.dot_general(
            pgrad[...], up[cols, :], nt, preferred_element_type=f32
        ).astype(bf16)
        for k in range(1, n_w):
            ww = lax.rem(w + k, n_w)
            send(npart.at[w_rows(ww), cols], nrecv.at[k, :, cols], r2_s.at[c, k], r2_r.at[c, k], at_wa(ww))
    for k in range(1, n_w):
        for c in range(width // step):
            arrived(nrecv.at[k, :, pl.ds(c * step, step)], r2_s.at[c, k], r2_r.at[c, k], at_wa(w))
    ngrad = npart[w_rows(w), :].astype(f32)
    for k in range(1, n_w):
        ngrad = ngrad + nrecv[k].astype(f32)
    back = norm_backward(ngrad, gain[...], normed[...], inv[:, 0:1])
    sg[w_rows(w), :] = (cot[w_rows(w), :].astype(f32) + back).astype(bf16)
    for k in range(1, n_w):
        send(sg.at[w_rows(w)], sg.at[w_rows(w)], a2_s.at[k], a2_r.at[k], at_wa(lax.rem(w + k, n_w)))
    for k in range(1, n_w):
        arrived(sg.at[w_rows(lax.rem(w + n_w - k, n_w))], a2_s.at[k], a2_r.at[k], at_wa(w))

    gmask[...] = (
        lax.dot_general(sg[...], ow[...], nt, preferred_element_type=f32).astype(bf16).astype(f32)
        * own_mark
    ).astype(bf16)

    def weight_tile(cols):
        wsend[cols, :] = lax.dot_general(sg[:, cols], att[...], tn, preferred_element_type=f32).astype(bf16)

    col_tiles(width, weight_tile)

    def send_weight():
        for k in range(1, n):
            idx, dev = group_peer(k)
            send(wsend.at[slab_rows(idx)], wrecv.at[k], wg_s.at[k], wg_r.at[k], dev)

    def back_head(e):
        cols = pl.ds(e * HS, HS)
        grad = gmask[:, cols]
        total[:, 0:1] = jnp.sum(grad.astype(f32) * mix[:, cols], axis=1, keepdims=True)
        mix[:, cols] = jnp.zeros((rows, HS), f32)

        def tile(slot):
            p = probs[e, slot]
            gp = lax.dot_general(gmask[:, cols], kv[slot, value_rows, cols], nt, preferred_element_type=f32)
            ds = (p.astype(f32) * (gp - total[:, 0:1]) * score_scale).astype(bf16)
            mix[:, cols] = mix[:, cols] + jnp.dot(ds, kv[slot, key_rows, cols], preferred_element_type=f32)
            psend[slot, key_rows, cols] = lax.dot_general(
                ds, q[:, cols], tn, preferred_element_type=f32
            ).astype(bf16)
            psend[slot, value_rows, cols] = lax.dot_general(
                p, gmask[:, cols], tn, preferred_element_type=f32
            ).astype(bf16)

        each_tile(tile)
        for slot in (0, 2, 6, 8, 1, 7, 3, 5):
            tt, hh = place(slot)
            send(
                psend.at[slot, :, cols], precv.at[8 - slot, :, cols],
                pt_s.at[e, slot], pt_r.at[e, 8 - slot], at_group(tt, hh), inside(tt, hh),
            )

    for e in range(heads):
        back_head(e)
        if e == 0:
            send_weight()
    qg[...] = mix[...].astype(bf16)
    wsum = wsend[slab_rows(g), :].astype(f32)
    for k in range(1, n):
        arrived(wrecv.at[k], wg_s.at[k], wg_r.at[k], at_group(t, h))
        wsum = wsum + wrecv[k].astype(f32)
    wg[...] = wsum
    for e in range(heads):
        cols = pl.ds(e * HS, HS)
        for slot in (0, 2, 6, 8, 1, 7, 3, 5):
            tt, hh = place(slot)
            arrived(precv.at[slot, :, cols], pt_s.at[e, slot], pt_r.at[e, slot], at_group(t, h), inside(tt, hh))
    act[:, pl.ds(0, channels)] = psend[CENTRE, key_rows, :].astype(f32)
    mix[...] = psend[CENTRE, value_rows, :].astype(f32)
    for slot in (0, 1, 2, 3, 5, 6, 7, 8):
        tt, hh = place(slot)

        def gather(slot=slot):
            act[:, pl.ds(0, channels)] = act[:, pl.ds(0, channels)] + precv[slot, key_rows, :].astype(f32)
            mix[...] = mix[...] + precv[slot, value_rows, :].astype(f32)

        pl.when(inside(tt, hh))(gather)
    kg[...] = act[:, pl.ds(0, channels)].astype(bf16)
    vg[...] = mix[...].astype(bf16)
    for copy, cond in pending:
        if cond is None:
            copy.wait_send()
        else:
            pl.when(cond)(copy.wait_send)


def fused_shards(
    stream, queries, key_heads, value_heads, out_weight, norm_gain, up_weight, down_weight,
    tile_route, cotangent,
):
    n_t, n_h, n_w = (lax.axis_size(a) for a in ("ta", "ha", "wa"))
    n = n_t * n_h
    rows, width = stream.shape[2:]
    channels = queries.shape[3]
    heads = channels // HS
    slab, hidden = up_weight.shape
    share = rows // n_w
    bf16, f32 = jnp.bfloat16, jnp.float32
    mark = jnp.broadcast_to(tile_route.reshape(1, 1).astype(bf16), (16, channels))
    kvm = jnp.concatenate([key_heads.reshape(rows, channels), value_heads.reshape(rows, channels), mark], axis=0)
    vm, dma = pltpu.VMEM, pltpu.SemaphoreType.DMA
    tiles = width // 512
    sg, qg, kg, vg, wg = pl.pallas_call(
        functools.partial(step_kernel, n_t, n_h, n_w),
        out_shape=[
            jax.ShapeDtypeStruct((rows, width), bf16),
            jax.ShapeDtypeStruct((rows, channels), bf16),
            jax.ShapeDtypeStruct((rows, channels), bf16),
            jax.ShapeDtypeStruct((rows, channels), bf16),
            jax.ShapeDtypeStruct((slab, channels), f32),
        ],
        in_specs=[pl.BlockSpec(memory_space=vm)] * 8,
        out_specs=[pl.BlockSpec(memory_space=vm)] * 5,
        scratch_shapes=[
            vm((WINDOW,) + kvm.shape, bf16),
            vm((width, hidden), bf16),
            vm((width, hidden), bf16),
            vm((WINDOW, TILE, TILE), f32),
            vm((rows, 128), f32),
            vm((rows, 128), f32),
            vm((heads, WINDOW, TILE, TILE), bf16),
            vm((rows, channels), f32),
            vm((rows, channels), bf16),
            vm((rows, width), bf16),
            vm((n_w, share, width), bf16),
            vm((rows, width), bf16),
            vm((share, width), f32),
            vm((share, 128), f32),
            vm((rows, hidden), f32),
            vm((rows, hidden), bf16),
            vm((rows, width), bf16),
            vm((n_w, share, width), bf16),
            vm((rows, channels), bf16),
            vm((width, channels), bf16),
            vm((n, slab, channels), bf16),
            vm((WINDOW, 2 * TILE, channels), bf16),
            vm((WINDOW, 2 * TILE, channels), bf16),
            dma((WINDOW,)), dma((WINDOW,)),
            dma((2, 4, n)), dma((2, n)),
            dma((n_w,)), dma((n_w,)), dma((n_w,)), dma((n_w,)),
            dma((tiles, n_w)), dma((tiles, n_w)), dma((n_w,)), dma((n_w,)),
            dma((n,)), dma((n,)),
            dma((heads, WINDOW)), dma((heads, WINDOW)),
        ],
        compiler_params=pltpu.CompilerParams(
            collective_id=0, has_side_effects=True, vmem_limit_bytes=62 * 1024 * 1024
        ),
    )(
        kvm, queries.reshape(rows, channels), stream.reshape(rows, width),
        cotangent.reshape(rows, width), out_weight, norm_gain.reshape(1, width),
        up_weight, down_weight.T,
    )
    cell = (1, 1, rows)
    return (
        sg.reshape(cell + (width,)),
        qg.reshape(cell + (channels,)),
        kg.reshape(cell + (channels,)),
        vg.reshape(cell + (channels,)),
        wg.T,
    )


def fits_kernel(mesh, stream, up_weight, tile_route):
    n = mesh.shape["ta"] * mesh.shape["ha"]
    slab = up_weight.shape[0] // n
    share = stream.shape[2] // mesh.shape["wa"]
    return slab % 16 == 0 and share % 16 == 0 and tile_route.shape[2] == 1 and stream.shape[3] % 512 == 0


def solution(mesh):
    placed = (
        P("ta", "ha", None, None),
        P("ta", "ha", None, "wa"),
        P("ta", "ha", None, "wa"),
        P("ta", "ha", None, "wa"),
        P("wa", None),
        P(),
        P(("ta", "ha"), "wa"),
        P("wa", ("ta", "ha")),
        P("ta", "ha", None),
        P("ta", "ha", None, None),
    )
    def run(*args):
        chosen = fused_shards if fits_kernel(mesh, args[0], args[6], args[8]) else shards
        return placed_call(chosen)(*args)

    placed_call = lambda body: jax.shard_map(
        body,
        mesh=mesh,
        in_specs=placed,
        out_specs=(
            P("ta", "ha", None, None),
            P("ta", "ha", None, "wa"),
            P("ta", "ha", None, "wa"),
            P("ta", "ha", None, "wa"),
            P("wa", ("ta", "ha")),
        ),
        check_vma=False,
    )

    return run
```

```python
import functools
import math

import jax
import jax.numpy as jnp
from jax import lax
from jax.experimental import pallas as pl
from jax.experimental.pallas import tpu as pltpu
from jax.sharding import PartitionSpec as P

HS = 128
TILE = 384


EPSILON = 1e-06
TANH_SCALE = 0.7978845608028654
CUBIC_COEF = 0.044715
NEG_FILL = -1e30


def extended(cells, sides, width):
    for axis, dim in sides:
        count = lax.axis_size(axis)
        ends = count - 1
        head = lax.slice_in_dim(cells, 0, width, axis=dim)
        tail = lax.slice_in_dim(cells, cells.shape[dim] - width, cells.shape[dim], axis=dim)
        cells = jnp.concatenate(
            [
                lax.ppermute(tail, axis, [(i, (i + 1) % count) for i in range(ends)]),
                cells,
                lax.ppermute(head, axis, [((i + 1) % count, i) for i in range(ends)]),
            ],
            axis=dim,
        )
    return cells


def from_behind(array, axis, by):
    devices = lax.axis_size(axis)
    pairs = [(i, i + by) for i in range(devices) if 0 <= i + by < devices]
    return lax.ppermute(array, axis, pairs)


def gelu_slope(pre_act):
    tanh_arg = TANH_SCALE * (pre_act + CUBIC_COEF * pre_act * pre_act * pre_act)
    tanh_val = jnp.tanh(tanh_arg)
    return 0.5 * (1.0 + tanh_val) + 0.5 * pre_act * (1.0 - tanh_val * tanh_val) * TANH_SCALE * (
        1.0 + 3.0 * CUBIC_COEF * pre_act * pre_act
    )


def head_probs(query_rows, key_rows, key_marks, score_scale):
    scores = (
        jnp.einsum("qd,kd->qk", query_rows, key_rows, preferred_element_type=jnp.float32)
        * score_scale
    )
    scores = jnp.where(key_marks[None, :] > 0.5, scores, NEG_FILL)
    row_max = jnp.max(scores, axis=1)
    weights = jnp.exp(scores - row_max[:, None])
    row_total = jnp.sum(weights, axis=1)
    return (weights / row_total[:, None], row_max, row_total)


def layer_norm(residual):
    mean_val = jnp.mean(residual, axis=1, keepdims=True)
    centered = residual - mean_val
    variance = jnp.mean(centered * centered, axis=1, keepdims=True)
    inv_std = lax.rsqrt(variance + EPSILON)
    return (centered * inv_std, inv_std)


def norm_backward(norm_grad, norm_gain, normed, inv_std):
    scaled = norm_grad * norm_gain
    return (
        scaled
        - jnp.mean(scaled, axis=1, keepdims=True)
        - normed * jnp.mean(scaled * normed, axis=1, keepdims=True)
    ) * inv_std


def shards(
    stream,
    queries,
    key_heads,
    value_heads,
    out_weight,
    norm_gain,
    up_weight,
    down_weight,
    tile_route,
    cotangent,
):
    row_count = stream.shape[2]
    model_width = stream.shape[3]
    channels = queries.shape[3]
    heads_here = channels // HS
    tile_count = row_count // TILE
    score_scale = 1.0 / math.sqrt(HS)
    tile_ids = jnp.arange(tile_count, dtype=jnp.int32)
    tile_marks = tile_route.astype(jnp.bfloat16)
    faces_key, faces_value, faces_marks = (
        extended(key_heads, (("ta", 0), ("ha", 1)), 1),
        extended(value_heads, (("ta", 0), ("ha", 1)), 1),
        extended(tile_marks, (("ta", 0), ("ha", 1)), 1),
    )

    def window():
        key_block = faces_key.reshape(9 * TILE, heads_here, HS)
        value_block = faces_value.reshape(9 * TILE, heads_here, HS)
        mark_block = faces_marks.reshape(9).astype(jnp.float32)
        key_marks = jnp.repeat(mark_block, TILE)
        query_tile = queries.reshape(TILE, heads_here, HS)
        return (
            query_tile.transpose(1, 0, 2),
            key_block.transpose(1, 0, 2),
            value_block.transpose(1, 0, 2),
            key_marks,
        )

    def forward_tile(tile_index):
        own_mark = tile_marks[0, 0, tile_index]
        query_tile, key_block, value_block, key_marks = window()

        def per_head(operands):
            query_rows, key_rows, value_rows = operands
            weights, row_max, row_total = head_probs(query_rows, key_rows, key_marks, score_scale)
            mixture = jnp.dot(
                weights.astype(jnp.bfloat16), value_rows, preferred_element_type=jnp.float32
            )
            return (mixture, row_max, row_total)

        mixture, row_max, row_total = lax.map(per_head, (query_tile, key_block, value_block))
        scaled = (mixture * own_mark.astype(jnp.float32)).astype(jnp.bfloat16)
        return (scaled.transpose(1, 0, 2).reshape(TILE, channels), row_max, row_total)

    attn_tiles, max_tiles, total_tiles = lax.map(forward_tile, tile_ids)
    attention = attn_tiles.reshape(row_count, channels)
    attn_part = jnp.dot(attention, out_weight, preferred_element_type=jnp.float32)
    head_share = lax.psum_scatter(attn_part, "wa", scatter_dimension=0, tiled=True)
    share_rows = head_share.shape[0]
    share_start = lax.axis_index("wa") * share_rows
    flat_stream = stream.reshape(row_count, model_width)
    flat_cot = cotangent.reshape(row_count, model_width)
    residual = (
        lax.dynamic_slice_in_dim(flat_stream, share_start, share_rows, 0).astype(jnp.float32)
        + head_share
    )
    normed, inv_std = layer_norm(residual)
    hidden_share = (normed * norm_gain).astype(jnp.bfloat16)
    hidden_in = lax.all_gather(hidden_share, "wa", axis=0, tiled=True)
    up_full, down_full = (
        lax.all_gather(up_weight, ("ta", "ha"), axis=0, tiled=True),
        lax.all_gather(down_weight, ("ta", "ha"), axis=1, tiled=True),
    )
    pre_act = jnp.dot(hidden_in, up_full, preferred_element_type=jnp.float32)
    act_grad = jnp.einsum("td,fd->tf", flat_cot, down_full, preferred_element_type=jnp.float32)
    pre_grad = (act_grad * gelu_slope(pre_act)).astype(jnp.bfloat16)
    norm_part = jnp.einsum("tf,df->td", pre_grad, up_full, preferred_element_type=jnp.float32)
    norm_share = lax.psum_scatter(norm_part, "wa", scatter_dimension=0, tiled=True)
    cot_share = lax.dynamic_slice_in_dim(flat_cot, share_start, share_rows, 0).astype(jnp.float32)
    grad_share = (cot_share + norm_backward(norm_share, norm_gain, normed, inv_std)).astype(
        jnp.bfloat16
    )
    stream_grad = lax.all_gather(grad_share, "wa", axis=0, tiled=True)
    weight_part = jnp.einsum(
        "tc,td->cd", attention, stream_grad, preferred_element_type=jnp.float32
    )
    out_weight_grad = lax.psum_scatter(weight_part, ("ta", "ha"), scatter_dimension=1, tiled=True)
    attn_grad = jnp.einsum(
        "td,cd->tc", stream_grad, out_weight, preferred_element_type=jnp.float32
    ).astype(jnp.bfloat16)
    row_marks = jnp.repeat(tile_marks.reshape(tile_count), TILE)
    masked_grad = attn_grad * row_marks[:, None]

    def own_side():
        query_tile, key_block, value_block, key_marks = window()
        grad_tile = masked_grad.reshape(TILE, heads_here, HS).transpose(1, 0, 2)

        def head_back(operands):
            query_rows, key_rows, value_rows, grad_rows = operands
            weights = head_probs(query_rows, key_rows, key_marks, score_scale)[0]
            grad_probs = jnp.einsum(
                "qd,kd->qk", grad_rows, value_rows, preferred_element_type=jnp.float32
            )
            row_delta = jnp.sum(weights * grad_probs, axis=1)
            grad_scores = (weights * (grad_probs - row_delta[:, None]) * score_scale).astype(
                jnp.bfloat16
            )
            query_part = jnp.dot(grad_scores, key_rows, preferred_element_type=jnp.float32).astype(
                jnp.bfloat16
            )
            value_part = jnp.einsum(
                "qk,qd->kd",
                weights.astype(jnp.bfloat16),
                grad_rows,
                preferred_element_type=jnp.float32,
            ).astype(jnp.bfloat16)
            key_part = jnp.einsum(
                "qk,qd->kd", grad_scores, query_rows, preferred_element_type=jnp.float32
            ).astype(jnp.bfloat16)
            return (query_part, row_delta, key_part, value_part)

        results = lax.map(head_back, (query_tile, key_block, value_block, grad_tile))
        query_part = results[0].transpose(1, 0, 2).reshape(TILE, channels)
        key_part = results[2].transpose(1, 0, 2).reshape(3, 3, TILE, channels)
        value_part = results[3].transpose(1, 0, 2).reshape(3, 3, TILE, channels)
        return (query_part, results[1], key_part, value_part)

    def guarded_own():
        blank_parts = (
            jnp.zeros((TILE, channels), jnp.bfloat16),
            jnp.zeros((heads_here, TILE), jnp.float32),
        )
        blank_parts = blank_parts + (
            jnp.zeros((3, 3, TILE, channels), jnp.bfloat16),
            jnp.zeros((3, 3, TILE, channels), jnp.bfloat16),
        )
        return own_side()

    def place_tile(carried, tile_index):
        query_part, row_delta, key_part, value_part = guarded_own()
        return ((key_part, value_part), query_part)

    empty_slots = jnp.zeros((3, 3, row_count, channels), jnp.bfloat16)
    (slots_key, slots_value), query_parts = lax.scan(
        place_tile, (empty_slots, empty_slots), tile_ids
    )
    middle_key = slots_key[1].astype(jnp.float32)
    middle_value = slots_value[1].astype(jnp.float32)
    for by_step, source in ((-1, 0), (1, 2)):
        moved_key, moved_value = from_behind(
            (slots_key[source], slots_value[source]), "ta", by_step
        )
        middle_key = middle_key + moved_key.astype(jnp.float32)
        middle_value = middle_value + moved_value.astype(jnp.float32)
    final_key = middle_key[1]
    final_value = middle_value[1]
    for by_step, source in ((-1, 0), (1, 2)):
        moved_key, moved_value = (
            from_behind(middle_key[source].astype(jnp.bfloat16), "ha", by_step).astype(jnp.float32),
            from_behind(middle_value[source].astype(jnp.bfloat16), "ha", by_step).astype(
                jnp.float32
            ),
        )
        final_key = final_key + moved_key
        final_value = final_value + moved_value
    key_grad = final_key.astype(jnp.bfloat16).reshape(1, 1, row_count, channels)
    value_grad = final_value.astype(jnp.bfloat16).reshape(1, 1, row_count, channels)
    query_grad = query_parts.reshape(1, 1, row_count, channels)
    return (
        stream_grad.reshape(1, 1, row_count, model_width),
        query_grad,
        key_grad,
        value_grad,
        out_weight_grad,
    )


MESH = pl.DeviceIdType.MESH
WINDOW = 9
CENTRE = 4


def step_kernel(
    n_t, n_h, n_w, kvm, q, stream, cot, ow, gain, upw, dnw,
    sg, qg, kg, vg, wg,
    kv, up, dn, score, top, total, probs, mix, att, apart, arecv, hid, normed, inv,
    act, pgrad, npart, nrecv, gmask, wsend, wrecv, psend, precv,
    halo_s, halo_r, wt_s, wt_r, r1_s, r1_r, a1_s, a1_r, r2_s, r2_r, a2_s, a2_r,
    wg_s, wg_r, pt_s, pt_r,
):
    f32, bf16 = jnp.float32, jnp.bfloat16
    t, h, w = lax.axis_index("ta"), lax.axis_index("ha"), lax.axis_index("wa")
    n = n_t * n_h
    g = t * n_h + h
    rows, width = stream.shape
    channels = q.shape[1]
    heads = channels // HS
    slab = upw.shape[0]
    share = rows // n_w
    hidden = upw.shape[1]
    score_scale = 1.0 / math.sqrt(HS)
    pending = []

    def at_group(tt, hh):
        return {"ta": tt, "ha": hh}

    def at_wa(ww):
        return {"wa": ww}

    def group_peer(k):
        idx = lax.rem(g + k, n)
        return idx, at_group(idx // n_h, lax.rem(idx, n_h))

    def send(src, dst, s_sem, r_sem, dev, cond=None):
        copy = pltpu.make_async_remote_copy(
            src_ref=src, dst_ref=dst, send_sem=s_sem, recv_sem=r_sem,
            device_id=dev, device_id_type=MESH,
        )
        if cond is None:
            copy.start()
        else:
            pl.when(cond)(copy.start)
        pending.append((copy, cond))

    def arrived(dst, s_sem, r_sem, dev, cond=None):
        copy = pltpu.make_async_remote_copy(
            src_ref=dst, dst_ref=dst, send_sem=s_sem, recv_sem=r_sem,
            device_id=dev, device_id_type=MESH,
        )
        if cond is None:
            copy.wait_recv()
        else:
            pl.when(cond)(copy.wait_recv)

    def inside(tt, hh):
        return (tt >= 0) & (tt < n_t) & (hh >= 0) & (hh < n_h)

    def place(slot):
        return t + slot // 3 - 1, h + slot % 3 - 1

    def w_rows(ww):
        return pl.ds(pl.multiple_of(ww * share, share), share)

    def slab_rows(idx):
        return pl.ds(pl.multiple_of(idx * slab, slab), slab)

    pair = w + 1 - 2 * lax.rem(w, 2)
    chips = n_w // 2

    def gather_start(buf, s_sem, r_sem):
        for k in range(1, chips):
            ww = lax.rem(w + 2 * k, n_w)
            send(buf.at[w_rows(w)], buf.at[w_rows(w)], s_sem.at[k], r_sem.at[k], at_wa(ww))
        send(buf.at[w_rows(w)], buf.at[w_rows(w)], s_sem.at[0], r_sem.at[0], at_wa(pair))

    def gather_end(buf, s_sem, r_sem):
        for k in range(1, chips):
            block = buf.at[w_rows(lax.rem(w + n_w - 2 * k, n_w))]
            arrived(block, s_sem.at[k], r_sem.at[k], at_wa(w))
            send(block, block, s_sem.at[chips + k], r_sem.at[chips + k], at_wa(pair))
        arrived(buf.at[w_rows(pair)], s_sem.at[0], r_sem.at[0], at_wa(w))
        for k in range(1, chips):
            block = buf.at[w_rows(lax.rem(pair + n_w - 2 * k, n_w))]
            arrived(block, s_sem.at[chips + k], r_sem.at[chips + k], at_wa(w))

    barrier = pltpu.get_barrier_semaphore()
    for k in range(1, n):
        pl.semaphore_signal(barrier, inc=1, device_id=group_peer(k)[1], device_id_type=MESH)
    for k in range(1, n_w):
        pl.semaphore_signal(barrier, inc=1, device_id=at_wa(lax.rem(w + k, n_w)), device_id_type=MESH)
    pl.semaphore_wait(barrier, n - 1 + n_w - 1)

    def window_send(src, slot, tt, hh, cond):
        send(src, kv.at[slot], halo_s.at[slot], halo_r.at[slot], at_group(tt, hh), cond)

    def window_wait(slot):
        tt, hh = place(slot)
        arrived(kv.at[slot], halo_s.at[slot], halo_r.at[slot], at_group(t, h), inside(tt, hh))

    window_send(kvm, 3, t, h + 1, inside(t, h + 1))
    window_send(kvm, 5, t, h - 1, inside(t, h - 1))
    window_send(kvm, 1, t + 1, h, inside(t + 1, h))
    window_send(kvm, 7, t - 1, h, inside(t - 1, h))

    weights = (dn, up)

    def hop(which, src_ref, idx, way):
        tt, hh = ((t + 1, h), (t - 1, h), (t, h + 1), (t, h - 1))[way]
        return (
            src_ref, weights[which].at[slab_rows(idx)], wt_s.at[which, way, idx],
            wt_r.at[which, idx], at_group(tt, hh),
        ), inside(tt, hh)

    def forward(which, src_ref, idx, ways, cond=None):
        for way in ways:
            args, here = hop(which, src_ref, idx, way)
            send(*args, here if cond is None else here & cond)

    forward(0, dnw, g, (2, 3))
    forward(1, upw, g, (2, 3))

    def relay(which, d):
        for sign, way in ((1, 0), (-1, 1)):
            tt = t - sign * d
            cond = inside(tt, h)
            idx = jnp.clip(tt, 0, n_t - 1) * n_h + h
            block = weights[which].at[slab_rows(idx)]
            arrived(block, wt_s.at[which, way, idx], wt_r.at[which, idx], at_group(t, h), cond)
            forward(which, block, idx, (2, 3, way), cond)

    def finish(which):
        for e in range(1, n_h):
            for sign, way in ((1, 2), (-1, 3)):
                hh = h - sign * e
                for d in range(-(n_t - 1), n_t):
                    tt = t + d
                    cond = inside(tt, hh)
                    idx = jnp.clip(tt, 0, n_t - 1) * n_h + jnp.clip(hh, 0, n_h - 1)
                    block = weights[which].at[slab_rows(idx)]
                    arrived(block, wt_s.at[which, way, idx], wt_r.at[which, idx], at_group(t, h), cond)
                    if e < n_h - 1:
                        forward(which, block, idx, (way,), cond)

    kv[CENTRE] = kvm[...]
    dn[slab_rows(g), :] = dnw[...]
    up[slab_rows(g), :] = upw[...]

    for j in (0, 2):
        window_wait(3 + j)
        here = inside(t, h + j - 1)
        window_send(kv.at[3 + j], j, t + 1, h, inside(t + 1, h) & here)
        window_send(kv.at[3 + j], 6 + j, t - 1, h, inside(t - 1, h) & here)
    forward(0, dnw, g, (0, 1))
    forward(1, upw, g, (0, 1))
    for slot in (1, 7, 0, 2, 6, 8):
        window_wait(slot)

    def each_tile(work):
        @pl.loop(0, WINDOW)
        def _(slot):
            tt, hh = place(slot)
            pl.when(inside(tt, hh))(lambda: work(slot))

    nt = (((1,), (1,)), ((), ()))
    tn = (((0,), (0,)), ((), ()))
    key_rows, value_rows = pl.ds(0, TILE), pl.ds(TILE, TILE)
    own_mark = kvm[pl.ds(2 * TILE, 1), :].astype(f32)

    def attend(e):
        cols = pl.ds(e * HS, HS)
        top[...] = jnp.full(top.shape, NEG_FILL, f32)
        total[...] = jnp.zeros(total.shape, f32)
        mix[:, cols] = jnp.zeros((rows, HS), f32)

        def raw(slot):
            s = lax.dot_general(q[:, cols], kv[slot, key_rows, cols], nt, preferred_element_type=f32)
            mark = kv[slot, pl.ds(2 * TILE, 1), :].astype(f32)
            s = jnp.where(mark > 0.5, s * score_scale, NEG_FILL)
            score[slot] = s
            top[...] = jnp.maximum(top[...], jnp.max(s, axis=1, keepdims=True))

        each_tile(raw)

        def expo(slot):
            p = jnp.exp(score[slot] - top[:, 0:1])
            score[slot] = p
            total[...] = total[...] + jnp.sum(p, axis=1, keepdims=True)

        each_tile(expo)
        total[...] = 1.0 / total[...]

        def blend(slot):
            p = (score[slot] * total[:, 0:1]).astype(bf16)
            probs[e, slot] = p
            mix[:, cols] = mix[:, cols] + jnp.dot(p, kv[slot, value_rows, cols], preferred_element_type=f32)

        each_tile(blend)

    for e in range(heads):
        attend(e)
        if e == heads - 2:
            relay(0, 1)
    att[...] = (mix[...] * own_mark).astype(bf16)
    step = 512

    def col_tiles(count, work):
        @pl.loop(0, count // step)
        def _(c):
            work(pl.ds(pl.multiple_of(c * step, step), step))

    def project(cols):
        apart[:, cols] = jnp.dot(att[...], ow[:, cols], preferred_element_type=f32).astype(bf16)

    col_tiles(width, project)
    for k in range(1, n_w):
        ww = lax.rem(w + k, n_w)
        send(apart.at[w_rows(ww)], arecv.at[k], r1_s.at[k], r1_r.at[k], at_wa(ww))
    relay(1, 1)
    resid = stream[w_rows(w), :].astype(f32) + apart[w_rows(w), :].astype(f32)
    for k in range(1, n_w):
        arrived(arecv.at[k], r1_s.at[k], r1_r.at[k], at_wa(w))
        resid = resid + arecv[k].astype(f32)
    centered = resid - jnp.mean(resid, axis=1, keepdims=True)
    istd = lax.rsqrt(jnp.mean(centered * centered, axis=1, keepdims=True) + EPSILON)
    inv[...] = jnp.broadcast_to(istd, inv.shape)
    normed[...] = centered * istd
    hid[w_rows(w), :] = (normed[...] * gain[...]).astype(bf16)
    gather_start(hid, a1_s, a1_r)
    for d in range(2, n_t):
        relay(0, d)
        relay(1, d)
    finish(0)

    def act_tile(cols):
        act[:, cols] = jnp.dot(cot[...], dn[:, cols], preferred_element_type=f32)

    col_tiles(hidden, act_tile)
    gather_end(hid, a1_s, a1_r)
    finish(1)

    def grad_tile(cols):
        pre = jnp.dot(hid[...], up[:, cols], preferred_element_type=f32)
        pgrad[:, cols] = (act[:, cols] * gelu_slope(pre)).astype(bf16)

    col_tiles(hidden, grad_tile)
    def pair_sums(c):
        cols = pl.ds(c * step, step)
        for k in range(chips - 1, -1, -1):
            block = nrecv.at[k, :, cols]
            arrived(block, r2_s.at[c, k], r2_r.at[c, k], at_wa(w))
            if k == 0:
                continue
            ww = lax.rem(w + 2 * k, n_w)
            both = npart[w_rows(ww), cols].astype(f32) + nrecv[k, :, cols].astype(f32)
            npart[w_rows(ww), cols] = both.astype(bf16)
            send(
                npart.at[w_rows(ww), cols], nrecv.at[chips + k, :, cols],
                r2_s.at[c, chips + k], r2_r.at[c, chips + k], at_wa(ww),
            )

    for c in range(width // step):
        cols = pl.ds(c * step, step)
        npart[:, cols] = lax.dot_general(
            pgrad[...], up[cols, :], nt, preferred_element_type=f32
        ).astype(bf16)
        for k in range(chips - 1, -1, -1):
            ww = lax.rem(pair + 2 * k, n_w)
            send(
                npart.at[w_rows(ww), cols], nrecv.at[k, :, cols],
                r2_s.at[c, k], r2_r.at[c, k], at_wa(pair),
            )
        if c >= 1:
            pair_sums(c - 1)
    pair_sums(width // step - 1)
    for k in range(1, chips):
        for c in range(width // step):
            at = chips + k
            arrived(nrecv.at[at, :, pl.ds(c * step, step)], r2_s.at[c, at], r2_r.at[c, at], at_wa(w))
    ngrad = npart[w_rows(w), :].astype(f32) + nrecv[0].astype(f32)
    for k in range(1, chips):
        ngrad = ngrad + nrecv[chips + k].astype(f32)
    back = norm_backward(ngrad, gain[...], normed[...], inv[:, 0:1])
    sg[w_rows(w), :] = (cot[w_rows(w), :].astype(f32) + back).astype(bf16)
    gather_start(sg, a2_s, a2_r)
    gather_end(sg, a2_s, a2_r)

    gmask[...] = (
        lax.dot_general(sg[...], ow[...], nt, preferred_element_type=f32).astype(bf16).astype(f32)
        * own_mark
    ).astype(bf16)

    def weight_tile(cols):
        wsend[cols, :] = lax.dot_general(sg[:, cols], att[...], tn, preferred_element_type=f32).astype(bf16)

    col_tiles(width, weight_tile)

    def send_weight():
        for k in range(1, n):
            idx, dev = group_peer(k)
            send(wsend.at[slab_rows(idx)], wrecv.at[k], wg_s.at[k], wg_r.at[k], dev)

    def back_head(e):
        cols = pl.ds(e * HS, HS)
        grad = gmask[:, cols]
        total[:, 0:1] = jnp.sum(grad.astype(f32) * mix[:, cols], axis=1, keepdims=True)
        mix[:, cols] = jnp.zeros((rows, HS), f32)

        def tile(slot):
            p = probs[e, slot]
            gp = lax.dot_general(gmask[:, cols], kv[slot, value_rows, cols], nt, preferred_element_type=f32)
            ds = (p.astype(f32) * (gp - total[:, 0:1]) * score_scale).astype(bf16)
            mix[:, cols] = mix[:, cols] + jnp.dot(ds, kv[slot, key_rows, cols], preferred_element_type=f32)
            psend[slot, key_rows, cols] = lax.dot_general(
                ds, q[:, cols], tn, preferred_element_type=f32
            ).astype(bf16)
            psend[slot, value_rows, cols] = lax.dot_general(
                p, gmask[:, cols], tn, preferred_element_type=f32
            ).astype(bf16)

        each_tile(tile)
        for j in (0, 2, 1):
            for i in (0, 2):
                tt, hh = t + i - 1, h + j - 1
                land = (2 - i) * 3 + j
                send(
                    psend.at[i * 3 + j, :, cols], precv.at[land, :, cols],
                    pt_s.at[e, land], pt_r.at[e, land], at_group(tt, h), inside(tt, hh),
                )

    def part_wait(e, slot):
        tt, hh = place(slot)
        block = precv.at[slot, :, pl.ds(e * HS, HS)]
        arrived(block, pt_s.at[e, slot], pt_r.at[e, slot], at_group(t, h), inside(tt, hh))

    def sum_time(e):
        cols = pl.ds(e * HS, HS)
        for j in (0, 2, 1):
            here = inside(t, h + j - 1)
            base = e * HS if j == 1 else 2 * channels
            gap = channels if j == 1 else HS
            key_acc, value_acc = pl.ds(base, HS), pl.ds(base + gap, HS)
            for i in (0, 2):
                part_wait(e, i * 3 + j)

            def begin():
                act[:, key_acc] = psend[3 + j, key_rows, cols].astype(f32)
                act[:, value_acc] = psend[3 + j, value_rows, cols].astype(f32)

            pl.when(here)(begin)
            for i in (0, 2):

                def add():
                    act[:, key_acc] = act[:, key_acc] + precv[i * 3 + j, key_rows, cols].astype(f32)
                    act[:, value_acc] = act[:, value_acc] + precv[i * 3 + j, value_rows, cols].astype(f32)

                pl.when(inside(t + i - 1, h + j - 1))(add)
            if j == 1:
                continue

            def settle():
                psend[3 + j, key_rows, cols] = act[:, key_acc].astype(bf16)
                psend[3 + j, value_rows, cols] = act[:, value_acc].astype(bf16)

            pl.when(here)(settle)
            send(
                psend.at[3 + j, :, cols], precv.at[5 - j, :, cols],
                pt_s.at[e, 5 - j], pt_r.at[e, 5 - j], at_group(t, h + j - 1), here,
            )

    send_weight()
    for e in range(heads):
        back_head(e)
        if e >= 1:
            sum_time(e - 1)
    qg[...] = mix[...].astype(bf16)
    sum_time(heads - 1)
    wsum = wsend[slab_rows(g), :].astype(f32)
    for k in range(1, n):
        arrived(wrecv.at[k], wg_s.at[k], wg_r.at[k], at_group(t, h))
        wsum = wsum + wrecv[k].astype(f32)
    wg[...] = wsum
    for slot in (3, 5):
        for e in range(heads):
            part_wait(e, slot)
        tt, hh = place(slot)

        def gather(slot=slot):
            both = pl.ds(channels, channels)
            act[:, pl.ds(0, channels)] = act[:, pl.ds(0, channels)] + precv[slot, key_rows, :].astype(f32)
            act[:, both] = act[:, both] + precv[slot, value_rows, :].astype(f32)

        pl.when(inside(tt, hh))(gather)
    kg[...] = act[:, pl.ds(0, channels)].astype(bf16)
    vg[...] = act[:, pl.ds(channels, channels)].astype(bf16)
    for copy, cond in pending:
        if cond is None:
            copy.wait_send()
        else:
            pl.when(cond)(copy.wait_send)


def fused_shards(
    stream, queries, key_heads, value_heads, out_weight, norm_gain, up_weight, down_weight,
    tile_route, cotangent,
):
    n_t, n_h, n_w = (lax.axis_size(a) for a in ("ta", "ha", "wa"))
    n = n_t * n_h
    rows, width = stream.shape[2:]
    channels = queries.shape[3]
    heads = channels // HS
    slab, hidden = up_weight.shape
    share = rows // n_w
    bf16, f32 = jnp.bfloat16, jnp.float32
    mark = jnp.broadcast_to(tile_route.reshape(1, 1).astype(bf16), (16, channels))
    kvm = jnp.concatenate([key_heads.reshape(rows, channels), value_heads.reshape(rows, channels), mark], axis=0)
    vm, dma = pltpu.VMEM, pltpu.SemaphoreType.DMA
    tiles = width // 512
    sg, qg, kg, vg, wg = pl.pallas_call(
        functools.partial(step_kernel, n_t, n_h, n_w),
        out_shape=[
            jax.ShapeDtypeStruct((rows, width), bf16),
            jax.ShapeDtypeStruct((rows, channels), bf16),
            jax.ShapeDtypeStruct((rows, channels), bf16),
            jax.ShapeDtypeStruct((rows, channels), bf16),
            jax.ShapeDtypeStruct((slab, channels), f32),
        ],
        in_specs=[pl.BlockSpec(memory_space=vm)] * 8,
        out_specs=[pl.BlockSpec(memory_space=vm)] * 5,
        scratch_shapes=[
            vm((WINDOW,) + kvm.shape, bf16),
            vm((width, hidden), bf16),
            vm((width, hidden), bf16),
            vm((WINDOW, TILE, TILE), f32),
            vm((rows, 128), f32),
            vm((rows, 128), f32),
            vm((heads, WINDOW, TILE, TILE), bf16),
            vm((rows, channels), f32),
            vm((rows, channels), bf16),
            vm((rows, width), bf16),
            vm((n_w, share, width), bf16),
            vm((rows, width), bf16),
            vm((share, width), f32),
            vm((share, 128), f32),
            vm((rows, hidden), f32),
            vm((rows, hidden), bf16),
            vm((rows, width), bf16),
            vm((n_w, share, width), bf16),
            vm((rows, channels), bf16),
            vm((width, channels), bf16),
            vm((n, slab, channels), bf16),
            vm((WINDOW, 2 * TILE, channels), bf16),
            vm((WINDOW, 2 * TILE, channels), bf16),
            dma((WINDOW,)), dma((WINDOW,)),
            dma((2, 4, n)), dma((2, n)),
            dma((n_w,)), dma((n_w,)), dma((n_w,)), dma((n_w,)),
            dma((tiles, n_w)), dma((tiles, n_w)), dma((n_w,)), dma((n_w,)),
            dma((n,)), dma((n,)),
            dma((heads, WINDOW)), dma((heads, WINDOW)),
        ],
        compiler_params=pltpu.CompilerParams(
            collective_id=0, has_side_effects=True, vmem_limit_bytes=62 * 1024 * 1024
        ),
    )(
        kvm, queries.reshape(rows, channels), stream.reshape(rows, width),
        cotangent.reshape(rows, width), out_weight, norm_gain.reshape(1, width),
        up_weight, down_weight.T,
    )
    cell = (1, 1, rows)
    return (
        sg.reshape(cell + (width,)),
        qg.reshape(cell + (channels,)),
        kg.reshape(cell + (channels,)),
        vg.reshape(cell + (channels,)),
        wg.T,
    )


def fits_kernel(mesh, stream, up_weight, tile_route):
    n = mesh.shape["ta"] * mesh.shape["ha"]
    slab = up_weight.shape[0] // n
    share = stream.shape[2] // mesh.shape["wa"]
    pairs = mesh.shape["wa"] % 2 == 0
    return pairs and slab % 16 == 0 and share % 16 == 0 and tile_route.shape[2] == 1 and stream.shape[3] % 512 == 0


def solution(mesh):
    placed = (
        P("ta", "ha", None, None),
        P("ta", "ha", None, "wa"),
        P("ta", "ha", None, "wa"),
        P("ta", "ha", None, "wa"),
        P("wa", None),
        P(),
        P(("ta", "ha"), "wa"),
        P("wa", ("ta", "ha")),
        P("ta", "ha", None),
        P("ta", "ha", None, None),
    )
    def run(*args):
        chosen = fused_shards if fits_kernel(mesh, args[0], args[6], args[8]) else shards
        return placed_call(chosen)(*args)

    placed_call = lambda body: jax.shard_map(
        body,
        mesh=mesh,
        in_specs=placed,
        out_specs=(
            P("ta", "ha", None, None),
            P("ta", "ha", None, "wa"),
            P("ta", "ha", None, "wa"),
            P("ta", "ha", None, "wa"),
            P("wa", ("ta", "ha")),
        ),
        check_vma=False,
    )

    return run
```

```python
import functools
import math

import jax
import jax.numpy as jnp
from jax import lax
from jax.experimental import pallas as pl
from jax.experimental.pallas import tpu as pltpu
from jax.sharding import PartitionSpec as P

HS = 128
TILE = 384


EPSILON = 1e-06
TANH_SCALE = 0.7978845608028654
CUBIC_COEF = 0.044715
NEG_FILL = -1e30


def extended(cells, sides, width):
    for axis, dim in sides:
        count = lax.axis_size(axis)
        ends = count - 1
        head = lax.slice_in_dim(cells, 0, width, axis=dim)
        tail = lax.slice_in_dim(cells, cells.shape[dim] - width, cells.shape[dim], axis=dim)
        cells = jnp.concatenate(
            [
                lax.ppermute(tail, axis, [(i, (i + 1) % count) for i in range(ends)]),
                cells,
                lax.ppermute(head, axis, [((i + 1) % count, i) for i in range(ends)]),
            ],
            axis=dim,
        )
    return cells


def from_behind(array, axis, by):
    devices = lax.axis_size(axis)
    pairs = [(i, i + by) for i in range(devices) if 0 <= i + by < devices]
    return lax.ppermute(array, axis, pairs)


def gelu_slope(pre_act):
    tanh_arg = TANH_SCALE * (pre_act + CUBIC_COEF * pre_act * pre_act * pre_act)
    tanh_val = jnp.tanh(tanh_arg)
    return 0.5 * (1.0 + tanh_val) + 0.5 * pre_act * (1.0 - tanh_val * tanh_val) * TANH_SCALE * (
        1.0 + 3.0 * CUBIC_COEF * pre_act * pre_act
    )


def head_probs(query_rows, key_rows, key_marks, score_scale):
    scores = (
        jnp.einsum("qd,kd->qk", query_rows, key_rows, preferred_element_type=jnp.float32)
        * score_scale
    )
    scores = jnp.where(key_marks[None, :] > 0.5, scores, NEG_FILL)
    row_max = jnp.max(scores, axis=1)
    weights = jnp.exp(scores - row_max[:, None])
    row_total = jnp.sum(weights, axis=1)
    return (weights / row_total[:, None], row_max, row_total)


def layer_norm(residual):
    mean_val = jnp.mean(residual, axis=1, keepdims=True)
    centered = residual - mean_val
    variance = jnp.mean(centered * centered, axis=1, keepdims=True)
    inv_std = lax.rsqrt(variance + EPSILON)
    return (centered * inv_std, inv_std)


def norm_backward(norm_grad, norm_gain, normed, inv_std):
    scaled = norm_grad * norm_gain
    return (
        scaled
        - jnp.mean(scaled, axis=1, keepdims=True)
        - normed * jnp.mean(scaled * normed, axis=1, keepdims=True)
    ) * inv_std


def shards(
    stream,
    queries,
    key_heads,
    value_heads,
    out_weight,
    norm_gain,
    up_weight,
    down_weight,
    tile_route,
    cotangent,
):
    row_count = stream.shape[2]
    model_width = stream.shape[3]
    channels = queries.shape[3]
    heads_here = channels // HS
    tile_count = row_count // TILE
    score_scale = 1.0 / math.sqrt(HS)
    tile_ids = jnp.arange(tile_count, dtype=jnp.int32)
    tile_marks = tile_route.astype(jnp.bfloat16)
    faces_key, faces_value, faces_marks = (
        extended(key_heads, (("ta", 0), ("ha", 1)), 1),
        extended(value_heads, (("ta", 0), ("ha", 1)), 1),
        extended(tile_marks, (("ta", 0), ("ha", 1)), 1),
    )

    def window():
        key_block = faces_key.reshape(9 * TILE, heads_here, HS)
        value_block = faces_value.reshape(9 * TILE, heads_here, HS)
        mark_block = faces_marks.reshape(9).astype(jnp.float32)
        key_marks = jnp.repeat(mark_block, TILE)
        query_tile = queries.reshape(TILE, heads_here, HS)
        return (
            query_tile.transpose(1, 0, 2),
            key_block.transpose(1, 0, 2),
            value_block.transpose(1, 0, 2),
            key_marks,
        )

    def forward_tile(tile_index):
        own_mark = tile_marks[0, 0, tile_index]
        query_tile, key_block, value_block, key_marks = window()

        def per_head(operands):
            query_rows, key_rows, value_rows = operands
            weights, row_max, row_total = head_probs(query_rows, key_rows, key_marks, score_scale)
            mixture = jnp.dot(
                weights.astype(jnp.bfloat16), value_rows, preferred_element_type=jnp.float32
            )
            return (mixture, row_max, row_total)

        mixture, row_max, row_total = lax.map(per_head, (query_tile, key_block, value_block))
        scaled = (mixture * own_mark.astype(jnp.float32)).astype(jnp.bfloat16)
        return (scaled.transpose(1, 0, 2).reshape(TILE, channels), row_max, row_total)

    attn_tiles, max_tiles, total_tiles = lax.map(forward_tile, tile_ids)
    attention = attn_tiles.reshape(row_count, channels)
    attn_part = jnp.dot(attention, out_weight, preferred_element_type=jnp.float32)
    head_share = lax.psum_scatter(attn_part, "wa", scatter_dimension=0, tiled=True)
    share_rows = head_share.shape[0]
    share_start = lax.axis_index("wa") * share_rows
    flat_stream = stream.reshape(row_count, model_width)
    flat_cot = cotangent.reshape(row_count, model_width)
    residual = (
        lax.dynamic_slice_in_dim(flat_stream, share_start, share_rows, 0).astype(jnp.float32)
        + head_share
    )
    normed, inv_std = layer_norm(residual)
    hidden_share = (normed * norm_gain).astype(jnp.bfloat16)
    hidden_in = lax.all_gather(hidden_share, "wa", axis=0, tiled=True)
    up_full, down_full = (
        lax.all_gather(up_weight, ("ta", "ha"), axis=0, tiled=True),
        lax.all_gather(down_weight, ("ta", "ha"), axis=1, tiled=True),
    )
    pre_act = jnp.dot(hidden_in, up_full, preferred_element_type=jnp.float32)
    act_grad = jnp.einsum("td,fd->tf", flat_cot, down_full, preferred_element_type=jnp.float32)
    pre_grad = (act_grad * gelu_slope(pre_act)).astype(jnp.bfloat16)
    norm_part = jnp.einsum("tf,df->td", pre_grad, up_full, preferred_element_type=jnp.float32)
    norm_share = lax.psum_scatter(norm_part, "wa", scatter_dimension=0, tiled=True)
    cot_share = lax.dynamic_slice_in_dim(flat_cot, share_start, share_rows, 0).astype(jnp.float32)
    grad_share = (cot_share + norm_backward(norm_share, norm_gain, normed, inv_std)).astype(
        jnp.bfloat16
    )
    stream_grad = lax.all_gather(grad_share, "wa", axis=0, tiled=True)
    weight_part = jnp.einsum(
        "tc,td->cd", attention, stream_grad, preferred_element_type=jnp.float32
    )
    out_weight_grad = lax.psum_scatter(weight_part, ("ta", "ha"), scatter_dimension=1, tiled=True)
    attn_grad = jnp.einsum(
        "td,cd->tc", stream_grad, out_weight, preferred_element_type=jnp.float32
    ).astype(jnp.bfloat16)
    row_marks = jnp.repeat(tile_marks.reshape(tile_count), TILE)
    masked_grad = attn_grad * row_marks[:, None]

    def own_side():
        query_tile, key_block, value_block, key_marks = window()
        grad_tile = masked_grad.reshape(TILE, heads_here, HS).transpose(1, 0, 2)

        def head_back(operands):
            query_rows, key_rows, value_rows, grad_rows = operands
            weights = head_probs(query_rows, key_rows, key_marks, score_scale)[0]
            grad_probs = jnp.einsum(
                "qd,kd->qk", grad_rows, value_rows, preferred_element_type=jnp.float32
            )
            row_delta = jnp.sum(weights * grad_probs, axis=1)
            grad_scores = (weights * (grad_probs - row_delta[:, None]) * score_scale).astype(
                jnp.bfloat16
            )
            query_part = jnp.dot(grad_scores, key_rows, preferred_element_type=jnp.float32).astype(
                jnp.bfloat16
            )
            value_part = jnp.einsum(
                "qk,qd->kd",
                weights.astype(jnp.bfloat16),
                grad_rows,
                preferred_element_type=jnp.float32,
            ).astype(jnp.bfloat16)
            key_part = jnp.einsum(
                "qk,qd->kd", grad_scores, query_rows, preferred_element_type=jnp.float32
            ).astype(jnp.bfloat16)
            return (query_part, row_delta, key_part, value_part)

        results = lax.map(head_back, (query_tile, key_block, value_block, grad_tile))
        query_part = results[0].transpose(1, 0, 2).reshape(TILE, channels)
        key_part = results[2].transpose(1, 0, 2).reshape(3, 3, TILE, channels)
        value_part = results[3].transpose(1, 0, 2).reshape(3, 3, TILE, channels)
        return (query_part, results[1], key_part, value_part)

    def guarded_own():
        blank_parts = (
            jnp.zeros((TILE, channels), jnp.bfloat16),
            jnp.zeros((heads_here, TILE), jnp.float32),
        )
        blank_parts = blank_parts + (
            jnp.zeros((3, 3, TILE, channels), jnp.bfloat16),
            jnp.zeros((3, 3, TILE, channels), jnp.bfloat16),
        )
        return own_side()

    def place_tile(carried, tile_index):
        query_part, row_delta, key_part, value_part = guarded_own()
        return ((key_part, value_part), query_part)

    empty_slots = jnp.zeros((3, 3, row_count, channels), jnp.bfloat16)
    (slots_key, slots_value), query_parts = lax.scan(
        place_tile, (empty_slots, empty_slots), tile_ids
    )
    middle_key = slots_key[1].astype(jnp.float32)
    middle_value = slots_value[1].astype(jnp.float32)
    for by_step, source in ((-1, 0), (1, 2)):
        moved_key, moved_value = from_behind(
            (slots_key[source], slots_value[source]), "ta", by_step
        )
        middle_key = middle_key + moved_key.astype(jnp.float32)
        middle_value = middle_value + moved_value.astype(jnp.float32)
    final_key = middle_key[1]
    final_value = middle_value[1]
    for by_step, source in ((-1, 0), (1, 2)):
        moved_key, moved_value = (
            from_behind(middle_key[source].astype(jnp.bfloat16), "ha", by_step).astype(jnp.float32),
            from_behind(middle_value[source].astype(jnp.bfloat16), "ha", by_step).astype(
                jnp.float32
            ),
        )
        final_key = final_key + moved_key
        final_value = final_value + moved_value
    key_grad = final_key.astype(jnp.bfloat16).reshape(1, 1, row_count, channels)
    value_grad = final_value.astype(jnp.bfloat16).reshape(1, 1, row_count, channels)
    query_grad = query_parts.reshape(1, 1, row_count, channels)
    return (
        stream_grad.reshape(1, 1, row_count, model_width),
        query_grad,
        key_grad,
        value_grad,
        out_weight_grad,
    )


MESH = pl.DeviceIdType.MESH
WINDOW = 9
CENTRE = 4


def step_kernel(
    n_t, n_h, n_w, kvm, q, stream, cot, ow, gain, upw, dnw,
    sg, qg, kg, vg, wg,
    kv, up, dn, score, top, total, probs, mix, att, apart, arecv, hid, normed, inv,
    act, pgrad, npart, nrecv, gmask, wsend, wrecv, psend, precv,
    halo_s, halo_r, wt_s, wt_r, r1_s, r1_r, a1_s, a1_r, r2_s, r2_r, a2_s, a2_r,
    wg_s, wg_r, pt_s, pt_r,
):
    f32, bf16 = jnp.float32, jnp.bfloat16
    t, h, w = lax.axis_index("ta"), lax.axis_index("ha"), lax.axis_index("wa")
    n = n_t * n_h
    g = t * n_h + h
    rows, width = stream.shape
    channels = q.shape[1]
    heads = channels // HS
    slab = upw.shape[0]
    share = rows // n_w
    hidden = upw.shape[1]
    score_scale = 1.0 / math.sqrt(HS)
    pending = []

    def at_group(tt, hh):
        return {"ta": tt, "ha": hh}

    def at_wa(ww):
        return {"wa": ww}

    def group_peer(k):
        idx = lax.rem(g + k, n)
        return idx, at_group(idx // n_h, lax.rem(idx, n_h))

    def send(src, dst, s_sem, r_sem, dev, cond=None):
        copy = pltpu.make_async_remote_copy(
            src_ref=src, dst_ref=dst, send_sem=s_sem, recv_sem=r_sem,
            device_id=dev, device_id_type=MESH,
        )
        if cond is None:
            copy.start()
        else:
            pl.when(cond)(copy.start)
        pending.append((copy, cond))

    def arrived(dst, s_sem, r_sem, dev, cond=None):
        copy = pltpu.make_async_remote_copy(
            src_ref=dst, dst_ref=dst, send_sem=s_sem, recv_sem=r_sem,
            device_id=dev, device_id_type=MESH,
        )
        if cond is None:
            copy.wait_recv()
        else:
            pl.when(cond)(copy.wait_recv)

    def inside(tt, hh):
        return (tt >= 0) & (tt < n_t) & (hh >= 0) & (hh < n_h)

    def place(slot):
        return t + slot // 3 - 1, h + slot % 3 - 1

    def w_rows(ww):
        return pl.ds(pl.multiple_of(ww * share, share), share)

    def slab_rows(idx):
        return pl.ds(pl.multiple_of(idx * slab, slab), slab)

    pair = w + 1 - 2 * lax.rem(w, 2)
    chips = n_w // 2

    def gather_start(buf, s_sem, r_sem):
        for k in range(1, chips):
            ww = lax.rem(w + 2 * k, n_w)
            send(buf.at[w_rows(w)], buf.at[w_rows(w)], s_sem.at[k], r_sem.at[k], at_wa(ww))
        send(buf.at[w_rows(w)], buf.at[w_rows(w)], s_sem.at[0], r_sem.at[0], at_wa(pair))

    def gather_end(buf, s_sem, r_sem):
        for k in range(1, chips):
            block = buf.at[w_rows(lax.rem(w + n_w - 2 * k, n_w))]
            arrived(block, s_sem.at[k], r_sem.at[k], at_wa(w))
            send(block, block, s_sem.at[chips + k], r_sem.at[chips + k], at_wa(pair))
        arrived(buf.at[w_rows(pair)], s_sem.at[0], r_sem.at[0], at_wa(w))
        for k in range(1, chips):
            block = buf.at[w_rows(lax.rem(pair + n_w - 2 * k, n_w))]
            arrived(block, s_sem.at[chips + k], r_sem.at[chips + k], at_wa(w))

    barrier = pltpu.get_barrier_semaphore()
    for k in range(1, n):
        pl.semaphore_signal(barrier, inc=1, device_id=group_peer(k)[1], device_id_type=MESH)
    for k in range(1, n_w):
        pl.semaphore_signal(barrier, inc=1, device_id=at_wa(lax.rem(w + k, n_w)), device_id_type=MESH)
    pl.semaphore_wait(barrier, n - 1 + n_w - 1)

    def window_send(src, slot, tt, hh, cond):
        send(src, kv.at[slot], halo_s.at[slot], halo_r.at[slot], at_group(tt, hh), cond)

    def window_wait(slot):
        tt, hh = place(slot)
        arrived(kv.at[slot], halo_s.at[slot], halo_r.at[slot], at_group(t, h), inside(tt, hh))

    window_send(kvm, 3, t, h + 1, inside(t, h + 1))
    window_send(kvm, 5, t, h - 1, inside(t, h - 1))

    weights = (dn, up)

    def hop(which, src_ref, idx, way):
        tt, hh = ((t + 1, h), (t - 1, h), (t, h + 1), (t, h - 1))[way]
        return (
            src_ref, weights[which].at[slab_rows(idx)], wt_s.at[which, way, idx],
            wt_r.at[which, idx], at_group(tt, hh),
        ), inside(tt, hh)

    def forward(which, src_ref, idx, ways, cond=None):
        for way in ways:
            args, here = hop(which, src_ref, idx, way)
            send(*args, here if cond is None else here & cond)

    forward(0, dnw, g, (0, 1, 2, 3))
    window_send(kvm, 1, t + 1, h, inside(t + 1, h))
    window_send(kvm, 7, t - 1, h, inside(t - 1, h))
    forward(1, upw, g, (2, 3))

    def relay(which, d):
        for sign, way in ((1, 0), (-1, 1)):
            tt = t - sign * d
            cond = inside(tt, h)
            idx = jnp.clip(tt, 0, n_t - 1) * n_h + h
            block = weights[which].at[slab_rows(idx)]
            arrived(block, wt_s.at[which, way, idx], wt_r.at[which, idx], at_group(t, h), cond)
            forward(which, block, idx, (2, 3, way), cond)

    def finish(which):
        for e in range(1, n_h):
            for sign, way in ((1, 2), (-1, 3)):
                hh = h - sign * e
                for d in range(-(n_t - 1), n_t):
                    tt = t + d
                    cond = inside(tt, hh)
                    idx = jnp.clip(tt, 0, n_t - 1) * n_h + jnp.clip(hh, 0, n_h - 1)
                    block = weights[which].at[slab_rows(idx)]
                    arrived(block, wt_s.at[which, way, idx], wt_r.at[which, idx], at_group(t, h), cond)
                    if e < n_h - 1:
                        forward(which, block, idx, (way,), cond)

    kv[CENTRE] = kvm[...]
    dn[slab_rows(g), :] = dnw[...]
    up[slab_rows(g), :] = upw[...]

    for j in (0, 2):
        window_wait(3 + j)
        here = inside(t, h + j - 1)
        window_send(kv.at[3 + j], j, t + 1, h, inside(t + 1, h) & here)
        window_send(kv.at[3 + j], 6 + j, t - 1, h, inside(t - 1, h) & here)
    forward(1, upw, g, (0, 1))
    relay(0, 1)
    for slot in (1, 7, 0, 2, 6, 8):
        window_wait(slot)

    def each_tile(work):
        @pl.loop(0, WINDOW)
        def _(slot):
            tt, hh = place(slot)
            pl.when(inside(tt, hh))(lambda: work(slot))

    nt = (((1,), (1,)), ((), ()))
    tn = (((0,), (0,)), ((), ()))
    key_rows, value_rows = pl.ds(0, TILE), pl.ds(TILE, TILE)
    own_mark = kvm[pl.ds(2 * TILE, 1), :].astype(f32)

    def attend(e):
        cols = pl.ds(e * HS, HS)
        top[...] = jnp.full(top.shape, NEG_FILL, f32)
        total[...] = jnp.zeros(total.shape, f32)
        mix[:, cols] = jnp.zeros((rows, HS), f32)

        def raw(slot):
            s = lax.dot_general(q[:, cols], kv[slot, key_rows, cols], nt, preferred_element_type=f32)
            mark = kv[slot, pl.ds(2 * TILE, 1), :].astype(f32)
            s = jnp.where(mark > 0.5, s * score_scale, NEG_FILL)
            score[slot] = s
            top[...] = jnp.maximum(top[...], jnp.max(s, axis=1, keepdims=True))

        each_tile(raw)

        def expo(slot):
            p = jnp.exp(score[slot] - top[:, 0:1])
            score[slot] = p
            total[...] = total[...] + jnp.sum(p, axis=1, keepdims=True)

        each_tile(expo)
        total[...] = 1.0 / total[...]

        def blend(slot):
            p = (score[slot] * total[:, 0:1]).astype(bf16)
            probs[e, slot] = p
            mix[:, cols] = mix[:, cols] + jnp.dot(p, kv[slot, value_rows, cols], preferred_element_type=f32)

        each_tile(blend)

    for e in range(heads):
        attend(e)
        if e == heads - 2:
            relay(1, 1)
    att[...] = (mix[...] * own_mark).astype(bf16)
    step = 512

    def col_tiles(count, work):
        @pl.loop(0, count // step)
        def _(c):
            work(pl.ds(pl.multiple_of(c * step, step), step))

    def project(cols):
        apart[:, cols] = jnp.dot(att[...], ow[:, cols], preferred_element_type=f32).astype(bf16)

    col_tiles(width, project)
    for k in range(1, n_w):
        ww = lax.rem(w + k, n_w)
        send(apart.at[w_rows(ww)], arecv.at[k], r1_s.at[k], r1_r.at[k], at_wa(ww))
    if n_t > 2:
        relay(0, 2)
    resid = stream[w_rows(w), :].astype(f32) + apart[w_rows(w), :].astype(f32)
    for k in range(1, n_w):
        arrived(arecv.at[k], r1_s.at[k], r1_r.at[k], at_wa(w))
        resid = resid + arecv[k].astype(f32)
    centered = resid - jnp.mean(resid, axis=1, keepdims=True)
    istd = lax.rsqrt(jnp.mean(centered * centered, axis=1, keepdims=True) + EPSILON)
    inv[...] = jnp.broadcast_to(istd, inv.shape)
    normed[...] = centered * istd
    hid[w_rows(w), :] = (normed[...] * gain[...]).astype(bf16)
    gather_start(hid, a1_s, a1_r)
    for d in range(2, n_t):
        if d > 2:
            relay(0, d)
        relay(1, d)
    finish(0)

    def act_tile(cols):
        act[:, cols] = jnp.dot(cot[...], dn[:, cols], preferred_element_type=f32)

    col_tiles(hidden, act_tile)
    gather_end(hid, a1_s, a1_r)
    finish(1)

    def grad_tile(cols):
        pre = jnp.dot(hid[...], up[:, cols], preferred_element_type=f32)
        pgrad[:, cols] = (act[:, cols] * gelu_slope(pre)).astype(bf16)

    col_tiles(hidden, grad_tile)
    def pair_sums(c):
        cols = pl.ds(c * step, step)
        for k in range(chips - 1, -1, -1):
            block = nrecv.at[k, :, cols]
            arrived(block, r2_s.at[c, k], r2_r.at[c, k], at_wa(w))
            if k == 0:
                continue
            ww = lax.rem(w + 2 * k, n_w)
            both = npart[w_rows(ww), cols].astype(f32) + nrecv[k, :, cols].astype(f32)
            npart[w_rows(ww), cols] = both.astype(bf16)
            send(
                npart.at[w_rows(ww), cols], nrecv.at[chips + k, :, cols],
                r2_s.at[c, chips + k], r2_r.at[c, chips + k], at_wa(ww),
            )

    for c in range(width // step):
        cols = pl.ds(c * step, step)
        npart[:, cols] = lax.dot_general(
            pgrad[...], up[cols, :], nt, preferred_element_type=f32
        ).astype(bf16)
        for k in range(chips - 1, -1, -1):
            ww = lax.rem(pair + 2 * k, n_w)
            send(
                npart.at[w_rows(ww), cols], nrecv.at[k, :, cols],
                r2_s.at[c, k], r2_r.at[c, k], at_wa(pair),
            )
        if c >= 1:
            pair_sums(c - 1)
    pair_sums(width // step - 1)
    for k in range(1, chips):
        for c in range(width // step):
            at = chips + k
            arrived(nrecv.at[at, :, pl.ds(c * step, step)], r2_s.at[c, at], r2_r.at[c, at], at_wa(w))
    ngrad = npart[w_rows(w), :].astype(f32) + nrecv[0].astype(f32)
    for k in range(1, chips):
        ngrad = ngrad + nrecv[chips + k].astype(f32)
    back = norm_backward(ngrad, gain[...], normed[...], inv[:, 0:1])
    sg[w_rows(w), :] = (cot[w_rows(w), :].astype(f32) + back).astype(bf16)
    gather_start(sg, a2_s, a2_r)
    gather_end(sg, a2_s, a2_r)

    gmask[...] = (
        lax.dot_general(sg[...], ow[...], nt, preferred_element_type=f32).astype(bf16).astype(f32)
        * own_mark
    ).astype(bf16)

    def weight_tile(cols):
        wsend[cols, :] = lax.dot_general(sg[:, cols], att[...], tn, preferred_element_type=f32).astype(bf16)

    col_tiles(width, weight_tile)

    late = (n_h - 1) * n_t

    def weight_slot(k, tt):
        return (k - 1) * n_t + tt

    def send_weight():
        for tt in range(n_t):
            for k in range(1, n_h):
                hh = lax.rem(h + k, n_h)
                at = weight_slot(k, tt)
                send(
                    wsend.at[slab_rows(tt * n_h + hh)], wrecv.at[at],
                    wg_s.at[at], wg_r.at[at], at_group(t, hh),
                )

    def height_sum(tt):
        both = wsend[slab_rows(tt * n_h + h), :].astype(f32)
        for k in range(1, n_h):
            both = both + wrecv[weight_slot(k, tt)].astype(f32)
        return both

    def relay_weight():
        for at in range(late):
            arrived(wrecv.at[at], wg_s.at[at], wg_r.at[at], at_group(t, h))
        for k in range(1, n_t):
            tt = lax.rem(t + k, n_t)
            block = slab_rows(tt * n_h + h)
            wsend[block, :] = height_sum(tt).astype(bf16)
            at = late + k - 1
            send(wsend.at[block], wrecv.at[at], wg_s.at[at], wg_r.at[at], at_group(tt, h))

    def back_head(e):
        cols = pl.ds(e * HS, HS)
        grad = gmask[:, cols]
        total[:, 0:1] = jnp.sum(grad.astype(f32) * mix[:, cols], axis=1, keepdims=True)
        mix[:, cols] = jnp.zeros((rows, HS), f32)

        def tile(slot):
            p = probs[e, slot]
            gp = lax.dot_general(gmask[:, cols], kv[slot, value_rows, cols], nt, preferred_element_type=f32)
            ds = (p.astype(f32) * (gp - total[:, 0:1]) * score_scale).astype(bf16)
            mix[:, cols] = mix[:, cols] + jnp.dot(ds, kv[slot, key_rows, cols], preferred_element_type=f32)
            psend[slot, key_rows, cols] = lax.dot_general(
                ds, q[:, cols], tn, preferred_element_type=f32
            ).astype(bf16)
            psend[slot, value_rows, cols] = lax.dot_general(
                p, gmask[:, cols], tn, preferred_element_type=f32
            ).astype(bf16)

        each_tile(tile)
        for j in (0, 2, 1):
            for i in (0, 2):
                tt, hh = t + i - 1, h + j - 1
                land = (2 - i) * 3 + j
                send(
                    psend.at[i * 3 + j, :, cols], precv.at[land, :, cols],
                    pt_s.at[e, land], pt_r.at[e, land], at_group(tt, h), inside(tt, hh),
                )

    def part_wait(e, slot):
        tt, hh = place(slot)
        block = precv.at[slot, :, pl.ds(e * HS, HS)]
        arrived(block, pt_s.at[e, slot], pt_r.at[e, slot], at_group(t, h), inside(tt, hh))

    def sum_time(e):
        cols = pl.ds(e * HS, HS)
        for j in (0, 2, 1):
            here = inside(t, h + j - 1)
            base = e * HS if j == 1 else 2 * channels
            gap = channels if j == 1 else HS
            key_acc, value_acc = pl.ds(base, HS), pl.ds(base + gap, HS)
            for i in (0, 2):
                part_wait(e, i * 3 + j)

            def begin():
                act[:, key_acc] = psend[3 + j, key_rows, cols].astype(f32)
                act[:, value_acc] = psend[3 + j, value_rows, cols].astype(f32)

            pl.when(here)(begin)
            for i in (0, 2):

                def add():
                    act[:, key_acc] = act[:, key_acc] + precv[i * 3 + j, key_rows, cols].astype(f32)
                    act[:, value_acc] = act[:, value_acc] + precv[i * 3 + j, value_rows, cols].astype(f32)

                pl.when(inside(t + i - 1, h + j - 1))(add)
            if j == 1:
                continue

            def settle():
                psend[3 + j, key_rows, cols] = act[:, key_acc].astype(bf16)
                psend[3 + j, value_rows, cols] = act[:, value_acc].astype(bf16)

            pl.when(here)(settle)
            send(
                psend.at[3 + j, :, cols], precv.at[5 - j, :, cols],
                pt_s.at[e, 5 - j], pt_r.at[e, 5 - j], at_group(t, h + j - 1), here,
            )

    send_weight()
    for e in range(heads):
        back_head(e)
    relay_weight()
    qg[...] = mix[...].astype(bf16)
    for e in range(heads):
        sum_time(e)
    wsum = height_sum(t)
    for at in range(late, late + n_t - 1):
        arrived(wrecv.at[at], wg_s.at[at], wg_r.at[at], at_group(t, h))
        wsum = wsum + wrecv[at].astype(f32)
    wg[...] = wsum
    for slot in (3, 5):
        for e in range(heads):
            part_wait(e, slot)
        tt, hh = place(slot)

        def gather(slot=slot):
            both = pl.ds(channels, channels)
            act[:, pl.ds(0, channels)] = act[:, pl.ds(0, channels)] + precv[slot, key_rows, :].astype(f32)
            act[:, both] = act[:, both] + precv[slot, value_rows, :].astype(f32)

        pl.when(inside(tt, hh))(gather)
    kg[...] = act[:, pl.ds(0, channels)].astype(bf16)
    vg[...] = act[:, pl.ds(channels, channels)].astype(bf16)
    for copy, cond in pending:
        if cond is None:
            copy.wait_send()
        else:
            pl.when(cond)(copy.wait_send)


def fused_shards(
    stream, queries, key_heads, value_heads, out_weight, norm_gain, up_weight, down_weight,
    tile_route, cotangent,
):
    n_t, n_h, n_w = (lax.axis_size(a) for a in ("ta", "ha", "wa"))
    n = n_t * n_h
    rows, width = stream.shape[2:]
    channels = queries.shape[3]
    heads = channels // HS
    slab, hidden = up_weight.shape
    share = rows // n_w
    bf16, f32 = jnp.bfloat16, jnp.float32
    mark = jnp.broadcast_to(tile_route.reshape(1, 1).astype(bf16), (16, channels))
    kvm = jnp.concatenate([key_heads.reshape(rows, channels), value_heads.reshape(rows, channels), mark], axis=0)
    vm, dma = pltpu.VMEM, pltpu.SemaphoreType.DMA
    tiles = width // 512
    sg, qg, kg, vg, wg = pl.pallas_call(
        functools.partial(step_kernel, n_t, n_h, n_w),
        out_shape=[
            jax.ShapeDtypeStruct((rows, width), bf16),
            jax.ShapeDtypeStruct((rows, channels), bf16),
            jax.ShapeDtypeStruct((rows, channels), bf16),
            jax.ShapeDtypeStruct((rows, channels), bf16),
            jax.ShapeDtypeStruct((slab, channels), f32),
        ],
        in_specs=[pl.BlockSpec(memory_space=vm)] * 8,
        out_specs=[pl.BlockSpec(memory_space=vm)] * 5,
        scratch_shapes=[
            vm((WINDOW,) + kvm.shape, bf16),
            vm((width, hidden), bf16),
            vm((width, hidden), bf16),
            vm((WINDOW, TILE, TILE), f32),
            vm((rows, 128), f32),
            vm((rows, 128), f32),
            vm((heads, WINDOW, TILE, TILE), bf16),
            vm((rows, channels), f32),
            vm((rows, channels), bf16),
            vm((rows, width), bf16),
            vm((n_w, share, width), bf16),
            vm((rows, width), bf16),
            vm((share, width), f32),
            vm((share, 128), f32),
            vm((rows, hidden), f32),
            vm((rows, hidden), bf16),
            vm((rows, width), bf16),
            vm((n_w, share, width), bf16),
            vm((rows, channels), bf16),
            vm((width, channels), bf16),
            vm((n, slab, channels), bf16),
            vm((WINDOW, 2 * TILE, channels), bf16),
            vm((WINDOW, 2 * TILE, channels), bf16),
            dma((WINDOW,)), dma((WINDOW,)),
            dma((2, 4, n)), dma((2, n)),
            dma((n_w,)), dma((n_w,)), dma((n_w,)), dma((n_w,)),
            dma((tiles, n_w)), dma((tiles, n_w)), dma((n_w,)), dma((n_w,)),
            dma((n,)), dma((n,)),
            dma((heads, WINDOW)), dma((heads, WINDOW)),
        ],
        compiler_params=pltpu.CompilerParams(
            collective_id=0, has_side_effects=True, vmem_limit_bytes=62 * 1024 * 1024
        ),
    )(
        kvm, queries.reshape(rows, channels), stream.reshape(rows, width),
        cotangent.reshape(rows, width), out_weight, norm_gain.reshape(1, width),
        up_weight, down_weight.T,
    )
    cell = (1, 1, rows)
    return (
        sg.reshape(cell + (width,)),
        qg.reshape(cell + (channels,)),
        kg.reshape(cell + (channels,)),
        vg.reshape(cell + (channels,)),
        wg.T,
    )


def fits_kernel(mesh, stream, up_weight, tile_route):
    n = mesh.shape["ta"] * mesh.shape["ha"]
    slab = up_weight.shape[0] // n
    share = stream.shape[2] // mesh.shape["wa"]
    pairs = mesh.shape["wa"] % 2 == 0
    return pairs and slab % 16 == 0 and share % 16 == 0 and tile_route.shape[2] == 1 and stream.shape[3] % 512 == 0


def solution(mesh):
    placed = (
        P("ta", "ha", None, None),
        P("ta", "ha", None, "wa"),
        P("ta", "ha", None, "wa"),
        P("ta", "ha", None, "wa"),
        P("wa", None),
        P(),
        P(("ta", "ha"), "wa"),
        P("wa", ("ta", "ha")),
        P("ta", "ha", None),
        P("ta", "ha", None, None),
    )
    def run(*args):
        chosen = fused_shards if fits_kernel(mesh, args[0], args[6], args[8]) else shards
        return placed_call(chosen)(*args)

    placed_call = lambda body: jax.shard_map(
        body,
        mesh=mesh,
        in_specs=placed,
        out_specs=(
            P("ta", "ha", None, None),
            P("ta", "ha", None, "wa"),
            P("ta", "ha", None, "wa"),
            P("ta", "ha", None, "wa"),
            P("wa", ("ta", "ha")),
        ),
        check_vma=False,
    )

    return run
```

```python
import functools
import math

import jax
import jax.numpy as jnp
from jax import lax
from jax.experimental import pallas as pl
from jax.experimental.pallas import tpu as pltpu
from jax.sharding import PartitionSpec as P

HS = 128
TILE = 384


EPSILON = 1e-06
TANH_SCALE = 0.7978845608028654
CUBIC_COEF = 0.044715
NEG_FILL = -1e30


def extended(cells, sides, width):
    for axis, dim in sides:
        count = lax.axis_size(axis)
        ends = count - 1
        head = lax.slice_in_dim(cells, 0, width, axis=dim)
        tail = lax.slice_in_dim(cells, cells.shape[dim] - width, cells.shape[dim], axis=dim)
        cells = jnp.concatenate(
            [
                lax.ppermute(tail, axis, [(i, (i + 1) % count) for i in range(ends)]),
                cells,
                lax.ppermute(head, axis, [((i + 1) % count, i) for i in range(ends)]),
            ],
            axis=dim,
        )
    return cells


def from_behind(array, axis, by):
    devices = lax.axis_size(axis)
    pairs = [(i, i + by) for i in range(devices) if 0 <= i + by < devices]
    return lax.ppermute(array, axis, pairs)


def gelu_slope(pre_act):
    tanh_arg = TANH_SCALE * (pre_act + CUBIC_COEF * pre_act * pre_act * pre_act)
    tanh_val = jnp.tanh(tanh_arg)
    return 0.5 * (1.0 + tanh_val) + 0.5 * pre_act * (1.0 - tanh_val * tanh_val) * TANH_SCALE * (
        1.0 + 3.0 * CUBIC_COEF * pre_act * pre_act
    )


def head_probs(query_rows, key_rows, key_marks, score_scale):
    scores = (
        jnp.einsum("qd,kd->qk", query_rows, key_rows, preferred_element_type=jnp.float32)
        * score_scale
    )
    scores = jnp.where(key_marks[None, :] > 0.5, scores, NEG_FILL)
    row_max = jnp.max(scores, axis=1)
    weights = jnp.exp(scores - row_max[:, None])
    row_total = jnp.sum(weights, axis=1)
    return (weights / row_total[:, None], row_max, row_total)


def layer_norm(residual):
    mean_val = jnp.mean(residual, axis=1, keepdims=True)
    centered = residual - mean_val
    variance = jnp.mean(centered * centered, axis=1, keepdims=True)
    inv_std = lax.rsqrt(variance + EPSILON)
    return (centered * inv_std, inv_std)


def norm_backward(norm_grad, norm_gain, normed, inv_std):
    scaled = norm_grad * norm_gain
    return (
        scaled
        - jnp.mean(scaled, axis=1, keepdims=True)
        - normed * jnp.mean(scaled * normed, axis=1, keepdims=True)
    ) * inv_std


def shards(
    stream,
    queries,
    key_heads,
    value_heads,
    out_weight,
    norm_gain,
    up_weight,
    down_weight,
    tile_route,
    cotangent,
):
    row_count = stream.shape[2]
    model_width = stream.shape[3]
    channels = queries.shape[3]
    heads_here = channels // HS
    tile_count = row_count // TILE
    score_scale = 1.0 / math.sqrt(HS)
    tile_ids = jnp.arange(tile_count, dtype=jnp.int32)
    tile_marks = tile_route.astype(jnp.bfloat16)
    faces_key, faces_value, faces_marks = (
        extended(key_heads, (("ta", 0), ("ha", 1)), 1),
        extended(value_heads, (("ta", 0), ("ha", 1)), 1),
        extended(tile_marks, (("ta", 0), ("ha", 1)), 1),
    )

    def window():
        key_block = faces_key.reshape(9 * TILE, heads_here, HS)
        value_block = faces_value.reshape(9 * TILE, heads_here, HS)
        mark_block = faces_marks.reshape(9).astype(jnp.float32)
        key_marks = jnp.repeat(mark_block, TILE)
        query_tile = queries.reshape(TILE, heads_here, HS)
        return (
            query_tile.transpose(1, 0, 2),
            key_block.transpose(1, 0, 2),
            value_block.transpose(1, 0, 2),
            key_marks,
        )

    def forward_tile(tile_index):
        own_mark = tile_marks[0, 0, tile_index]
        query_tile, key_block, value_block, key_marks = window()

        def per_head(operands):
            query_rows, key_rows, value_rows = operands
            weights, row_max, row_total = head_probs(query_rows, key_rows, key_marks, score_scale)
            mixture = jnp.dot(
                weights.astype(jnp.bfloat16), value_rows, preferred_element_type=jnp.float32
            )
            return (mixture, row_max, row_total)

        mixture, row_max, row_total = lax.map(per_head, (query_tile, key_block, value_block))
        scaled = (mixture * own_mark.astype(jnp.float32)).astype(jnp.bfloat16)
        return (scaled.transpose(1, 0, 2).reshape(TILE, channels), row_max, row_total)

    attn_tiles, max_tiles, total_tiles = lax.map(forward_tile, tile_ids)
    attention = attn_tiles.reshape(row_count, channels)
    attn_part = jnp.dot(attention, out_weight, preferred_element_type=jnp.float32)
    head_share = lax.psum_scatter(attn_part, "wa", scatter_dimension=0, tiled=True)
    share_rows = head_share.shape[0]
    share_start = lax.axis_index("wa") * share_rows
    flat_stream = stream.reshape(row_count, model_width)
    flat_cot = cotangent.reshape(row_count, model_width)
    residual = (
        lax.dynamic_slice_in_dim(flat_stream, share_start, share_rows, 0).astype(jnp.float32)
        + head_share
    )
    normed, inv_std = layer_norm(residual)
    hidden_share = (normed * norm_gain).astype(jnp.bfloat16)
    hidden_in = lax.all_gather(hidden_share, "wa", axis=0, tiled=True)
    up_full, down_full = (
        lax.all_gather(up_weight, ("ta", "ha"), axis=0, tiled=True),
        lax.all_gather(down_weight, ("ta", "ha"), axis=1, tiled=True),
    )
    pre_act = jnp.dot(hidden_in, up_full, preferred_element_type=jnp.float32)
    act_grad = jnp.einsum("td,fd->tf", flat_cot, down_full, preferred_element_type=jnp.float32)
    pre_grad = (act_grad * gelu_slope(pre_act)).astype(jnp.bfloat16)
    norm_part = jnp.einsum("tf,df->td", pre_grad, up_full, preferred_element_type=jnp.float32)
    norm_share = lax.psum_scatter(norm_part, "wa", scatter_dimension=0, tiled=True)
    cot_share = lax.dynamic_slice_in_dim(flat_cot, share_start, share_rows, 0).astype(jnp.float32)
    grad_share = (cot_share + norm_backward(norm_share, norm_gain, normed, inv_std)).astype(
        jnp.bfloat16
    )
    stream_grad = lax.all_gather(grad_share, "wa", axis=0, tiled=True)
    weight_part = jnp.einsum(
        "tc,td->cd", attention, stream_grad, preferred_element_type=jnp.float32
    )
    out_weight_grad = lax.psum_scatter(weight_part, ("ta", "ha"), scatter_dimension=1, tiled=True)
    attn_grad = jnp.einsum(
        "td,cd->tc", stream_grad, out_weight, preferred_element_type=jnp.float32
    ).astype(jnp.bfloat16)
    row_marks = jnp.repeat(tile_marks.reshape(tile_count), TILE)
    masked_grad = attn_grad * row_marks[:, None]

    def own_side():
        query_tile, key_block, value_block, key_marks = window()
        grad_tile = masked_grad.reshape(TILE, heads_here, HS).transpose(1, 0, 2)

        def head_back(operands):
            query_rows, key_rows, value_rows, grad_rows = operands
            weights = head_probs(query_rows, key_rows, key_marks, score_scale)[0]
            grad_probs = jnp.einsum(
                "qd,kd->qk", grad_rows, value_rows, preferred_element_type=jnp.float32
            )
            row_delta = jnp.sum(weights * grad_probs, axis=1)
            grad_scores = (weights * (grad_probs - row_delta[:, None]) * score_scale).astype(
                jnp.bfloat16
            )
            query_part = jnp.dot(grad_scores, key_rows, preferred_element_type=jnp.float32).astype(
                jnp.bfloat16
            )
            value_part = jnp.einsum(
                "qk,qd->kd",
                weights.astype(jnp.bfloat16),
                grad_rows,
                preferred_element_type=jnp.float32,
            ).astype(jnp.bfloat16)
            key_part = jnp.einsum(
                "qk,qd->kd", grad_scores, query_rows, preferred_element_type=jnp.float32
            ).astype(jnp.bfloat16)
            return (query_part, row_delta, key_part, value_part)

        results = lax.map(head_back, (query_tile, key_block, value_block, grad_tile))
        query_part = results[0].transpose(1, 0, 2).reshape(TILE, channels)
        key_part = results[2].transpose(1, 0, 2).reshape(3, 3, TILE, channels)
        value_part = results[3].transpose(1, 0, 2).reshape(3, 3, TILE, channels)
        return (query_part, results[1], key_part, value_part)

    def guarded_own():
        blank_parts = (
            jnp.zeros((TILE, channels), jnp.bfloat16),
            jnp.zeros((heads_here, TILE), jnp.float32),
        )
        blank_parts = blank_parts + (
            jnp.zeros((3, 3, TILE, channels), jnp.bfloat16),
            jnp.zeros((3, 3, TILE, channels), jnp.bfloat16),
        )
        return own_side()

    def place_tile(carried, tile_index):
        query_part, row_delta, key_part, value_part = guarded_own()
        return ((key_part, value_part), query_part)

    empty_slots = jnp.zeros((3, 3, row_count, channels), jnp.bfloat16)
    (slots_key, slots_value), query_parts = lax.scan(
        place_tile, (empty_slots, empty_slots), tile_ids
    )
    middle_key = slots_key[1].astype(jnp.float32)
    middle_value = slots_value[1].astype(jnp.float32)
    for by_step, source in ((-1, 0), (1, 2)):
        moved_key, moved_value = from_behind(
            (slots_key[source], slots_value[source]), "ta", by_step
        )
        middle_key = middle_key + moved_key.astype(jnp.float32)
        middle_value = middle_value + moved_value.astype(jnp.float32)
    final_key = middle_key[1]
    final_value = middle_value[1]
    for by_step, source in ((-1, 0), (1, 2)):
        moved_key, moved_value = (
            from_behind(middle_key[source].astype(jnp.bfloat16), "ha", by_step).astype(jnp.float32),
            from_behind(middle_value[source].astype(jnp.bfloat16), "ha", by_step).astype(
                jnp.float32
            ),
        )
        final_key = final_key + moved_key
        final_value = final_value + moved_value
    key_grad = final_key.astype(jnp.bfloat16).reshape(1, 1, row_count, channels)
    value_grad = final_value.astype(jnp.bfloat16).reshape(1, 1, row_count, channels)
    query_grad = query_parts.reshape(1, 1, row_count, channels)
    return (
        stream_grad.reshape(1, 1, row_count, model_width),
        query_grad,
        key_grad,
        value_grad,
        out_weight_grad,
    )


MESH = pl.DeviceIdType.MESH
WINDOW = 9
CENTRE = 4


def step_kernel(
    n_t, n_h, n_w, keys, values, route, q, stream, cot, ow, gain, upw, dnw,
    sg, qg, kg, vg, wg,
    kv, up, dn, score, top, total, probs, mix, att, apart, arecv, hid, normed, inv,
    act, pgrad, npart, nrecv, gmask, wsend, wrecv, psend, precv,
    halo_s, halo_r, wt_s, wt_r, r1_s, r1_r, a1_s, a1_r, r2_s, r2_r, a2_s, a2_r,
    wg_s, wg_r, pt_s, pt_r,
):
    f32, bf16 = jnp.float32, jnp.bfloat16
    t, h, w = lax.axis_index("ta"), lax.axis_index("ha"), lax.axis_index("wa")
    n = n_t * n_h
    g = t * n_h + h
    rows, width = stream.shape
    channels = q.shape[1]
    heads = channels // HS
    slab = upw.shape[0]
    share = rows // n_w
    hidden = upw.shape[1]
    score_scale = 1.0 / math.sqrt(HS)
    pending = []

    def at_group(tt, hh):
        return {"ta": tt, "ha": hh}

    def at_wa(ww):
        return {"wa": ww}

    def group_peer(k):
        idx = lax.rem(g + k, n)
        return idx, at_group(idx // n_h, lax.rem(idx, n_h))

    def send(src, dst, s_sem, r_sem, dev, cond=None):
        copy = pltpu.make_async_remote_copy(
            src_ref=src, dst_ref=dst, send_sem=s_sem, recv_sem=r_sem,
            device_id=dev, device_id_type=MESH,
        )
        if cond is None:
            copy.start()
        else:
            pl.when(cond)(copy.start)
        pending.append((copy, cond))

    def arrived(dst, s_sem, r_sem, dev, cond=None):
        copy = pltpu.make_async_remote_copy(
            src_ref=dst, dst_ref=dst, send_sem=s_sem, recv_sem=r_sem,
            device_id=dev, device_id_type=MESH,
        )
        if cond is None:
            copy.wait_recv()
        else:
            pl.when(cond)(copy.wait_recv)

    def inside(tt, hh):
        return (tt >= 0) & (tt < n_t) & (hh >= 0) & (hh < n_h)

    def place(slot):
        return t + slot // 3 - 1, h + slot % 3 - 1

    def w_rows(ww):
        return pl.ds(pl.multiple_of(ww * share, share), share)

    def slab_rows(idx):
        return pl.ds(pl.multiple_of(idx * slab, slab), slab)

    pair = w + 1 - 2 * lax.rem(w, 2)
    chips = n_w // 2

    def gather_start(buf, s_sem, r_sem):
        for k in range(1, chips):
            ww = lax.rem(w + 2 * k, n_w)
            send(buf.at[w_rows(w)], buf.at[w_rows(w)], s_sem.at[k], r_sem.at[k], at_wa(ww))
        send(buf.at[w_rows(w)], buf.at[w_rows(w)], s_sem.at[0], r_sem.at[0], at_wa(pair))

    def gather_end(buf, s_sem, r_sem):
        for k in range(1, chips):
            block = buf.at[w_rows(lax.rem(w + n_w - 2 * k, n_w))]
            arrived(block, s_sem.at[k], r_sem.at[k], at_wa(w))
            send(block, block, s_sem.at[chips + k], r_sem.at[chips + k], at_wa(pair))
        arrived(buf.at[w_rows(pair)], s_sem.at[0], r_sem.at[0], at_wa(w))
        for k in range(1, chips):
            block = buf.at[w_rows(lax.rem(pair + n_w - 2 * k, n_w))]
            arrived(block, s_sem.at[chips + k], r_sem.at[chips + k], at_wa(w))

    kvm = kv.at[CENTRE]
    kv[CENTRE, pl.ds(0, TILE), :] = keys[...]
    kv[CENTRE, pl.ds(TILE, TILE), :] = values[...]
    own = jnp.full((16, channels), route[0, 0, 0], jnp.int32).astype(f32)
    kv[CENTRE, pl.ds(2 * TILE, 16), :] = own.astype(bf16)
    barrier = pltpu.get_barrier_semaphore()
    for k in range(1, n):
        pl.semaphore_signal(barrier, inc=1, device_id=group_peer(k)[1], device_id_type=MESH)
    for k in range(1, n_w):
        pl.semaphore_signal(barrier, inc=1, device_id=at_wa(lax.rem(w + k, n_w)), device_id_type=MESH)
    pl.semaphore_wait(barrier, n - 1 + n_w - 1)

    def window_send(src, slot, tt, hh, cond):
        send(src, kv.at[slot], halo_s.at[slot], halo_r.at[slot], at_group(tt, hh), cond)

    def window_wait(slot):
        tt, hh = place(slot)
        arrived(kv.at[slot], halo_s.at[slot], halo_r.at[slot], at_group(t, h), inside(tt, hh))

    window_send(kvm, 3, t, h + 1, inside(t, h + 1))
    window_send(kvm, 5, t, h - 1, inside(t, h - 1))

    weights = (dn, up)

    def hop(which, src_ref, idx, way):
        tt, hh = ((t + 1, h), (t - 1, h), (t, h + 1), (t, h - 1))[way]
        return (
            src_ref, weights[which].at[slab_rows(idx)], wt_s.at[which, way, idx],
            wt_r.at[which, idx], at_group(tt, hh),
        ), inside(tt, hh)

    def forward(which, src_ref, idx, ways, cond=None):
        for way in ways:
            args, here = hop(which, src_ref, idx, way)
            send(*args, here if cond is None else here & cond)

    forward(0, dnw, g, (0, 1, 2, 3))
    window_send(kvm, 1, t + 1, h, inside(t + 1, h))
    window_send(kvm, 7, t - 1, h, inside(t - 1, h))
    forward(1, upw, g, (2, 3))

    def relay(which, d):
        for sign, way in ((1, 0), (-1, 1)):
            tt = t - sign * d
            cond = inside(tt, h)
            idx = jnp.clip(tt, 0, n_t - 1) * n_h + h
            block = weights[which].at[slab_rows(idx)]
            arrived(block, wt_s.at[which, way, idx], wt_r.at[which, idx], at_group(t, h), cond)
            forward(which, block, idx, (2, 3, way), cond)

    def finish(which):
        for e in range(1, n_h):
            for sign, way in ((1, 2), (-1, 3)):
                hh = h - sign * e
                for d in range(-(n_t - 1), n_t):
                    tt = t + d
                    cond = inside(tt, hh)
                    idx = jnp.clip(tt, 0, n_t - 1) * n_h + jnp.clip(hh, 0, n_h - 1)
                    block = weights[which].at[slab_rows(idx)]
                    arrived(block, wt_s.at[which, way, idx], wt_r.at[which, idx], at_group(t, h), cond)
                    if e < n_h - 1:
                        forward(which, block, idx, (way,), cond)

    dn[slab_rows(g), :] = dnw[...]
    up[slab_rows(g), :] = upw[...]

    for j in (0, 2):
        window_wait(3 + j)
        here = inside(t, h + j - 1)
        window_send(kv.at[3 + j], j, t + 1, h, inside(t + 1, h) & here)
        window_send(kv.at[3 + j], 6 + j, t - 1, h, inside(t - 1, h) & here)
    forward(1, upw, g, (0, 1))
    relay(0, 1)
    for slot in (1, 7, 0, 2, 6, 8):
        window_wait(slot)

    def each_tile(work):
        @pl.loop(0, WINDOW)
        def _(slot):
            tt, hh = place(slot)
            pl.when(inside(tt, hh))(lambda: work(slot))

    nt = (((1,), (1,)), ((), ()))
    tn = (((0,), (0,)), ((), ()))
    key_rows, value_rows = pl.ds(0, TILE), pl.ds(TILE, TILE)
    own_mark = kv[CENTRE, pl.ds(2 * TILE, 1), :].astype(f32)

    def attend(e):
        cols = pl.ds(e * HS, HS)
        top[...] = jnp.full(top.shape, NEG_FILL, f32)
        total[...] = jnp.zeros(total.shape, f32)
        mix[:, cols] = jnp.zeros((rows, HS), f32)

        def raw(slot):
            s = lax.dot_general(q[:, cols], kv[slot, key_rows, cols], nt, preferred_element_type=f32)
            mark = kv[slot, pl.ds(2 * TILE, 1), :].astype(f32)
            s = jnp.where(mark > 0.5, s * score_scale, NEG_FILL)
            score[slot] = s
            top[...] = jnp.maximum(top[...], jnp.max(s, axis=1, keepdims=True))

        each_tile(raw)

        def expo(slot):
            p = jnp.exp(score[slot] - top[:, 0:1])
            score[slot] = p
            total[...] = total[...] + jnp.sum(p, axis=1, keepdims=True)

        each_tile(expo)
        total[...] = 1.0 / total[...]

        def blend(slot):
            p = (score[slot] * total[:, 0:1]).astype(bf16)
            probs[e, slot] = p
            mix[:, cols] = mix[:, cols] + jnp.dot(p, kv[slot, value_rows, cols], preferred_element_type=f32)

        each_tile(blend)

    for e in range(heads):
        attend(e)
        if e == heads - 2:
            relay(1, 1)
    att[...] = (mix[...] * own_mark).astype(bf16)
    step = 512

    def col_tiles(count, work):
        @pl.loop(0, count // step)
        def _(c):
            work(pl.ds(pl.multiple_of(c * step, step), step))

    def project(cols):
        apart[:, cols] = jnp.dot(att[...], ow[:, cols], preferred_element_type=f32).astype(bf16)

    col_tiles(width, project)
    for k in range(1, n_w):
        ww = lax.rem(w + k, n_w)
        send(apart.at[w_rows(ww)], arecv.at[k], r1_s.at[k], r1_r.at[k], at_wa(ww))
    if n_t > 2:
        relay(0, 2)
    resid = stream[w_rows(w), :].astype(f32) + apart[w_rows(w), :].astype(f32)
    for k in range(1, n_w):
        arrived(arecv.at[k], r1_s.at[k], r1_r.at[k], at_wa(w))
        resid = resid + arecv[k].astype(f32)
    centered = resid - jnp.mean(resid, axis=1, keepdims=True)
    istd = lax.rsqrt(jnp.mean(centered * centered, axis=1, keepdims=True) + EPSILON)
    inv[...] = jnp.broadcast_to(istd, inv.shape)
    normed[...] = centered * istd
    hid[w_rows(w), :] = (normed[...] * gain[...].reshape(1, width)).astype(bf16)
    gather_start(hid, a1_s, a1_r)
    for d in range(2, n_t):
        if d > 2:
            relay(0, d)
        relay(1, d)
    finish(0)

    def act_tile(cols):
        act[:, cols] = jnp.dot(cot[...], dn[:, cols], preferred_element_type=f32)

    col_tiles(hidden, act_tile)
    gather_end(hid, a1_s, a1_r)
    finish(1)

    def grad_tile(cols):
        pre = jnp.dot(hid[...], up[:, cols], preferred_element_type=f32)
        pgrad[:, cols] = (act[:, cols] * gelu_slope(pre)).astype(bf16)

    col_tiles(hidden, grad_tile)
    def pair_sums(c):
        cols = pl.ds(c * step, step)
        for k in range(chips - 1, -1, -1):
            block = nrecv.at[k, :, cols]
            arrived(block, r2_s.at[c, k], r2_r.at[c, k], at_wa(w))
            if k == 0:
                continue
            ww = lax.rem(w + 2 * k, n_w)
            both = npart[w_rows(ww), cols].astype(f32) + nrecv[k, :, cols].astype(f32)
            npart[w_rows(ww), cols] = both.astype(bf16)
            send(
                npart.at[w_rows(ww), cols], nrecv.at[chips + k, :, cols],
                r2_s.at[c, chips + k], r2_r.at[c, chips + k], at_wa(ww),
            )

    for c in range(width // step):
        cols = pl.ds(c * step, step)
        npart[:, cols] = lax.dot_general(
            pgrad[...], up[cols, :], nt, preferred_element_type=f32
        ).astype(bf16)
        for k in range(chips - 1, -1, -1):
            ww = lax.rem(pair + 2 * k, n_w)
            send(
                npart.at[w_rows(ww), cols], nrecv.at[k, :, cols],
                r2_s.at[c, k], r2_r.at[c, k], at_wa(pair),
            )
        if c >= 1:
            pair_sums(c - 1)
    pair_sums(width // step - 1)
    for k in range(1, chips):
        for c in range(width // step):
            at = chips + k
            arrived(nrecv.at[at, :, pl.ds(c * step, step)], r2_s.at[c, at], r2_r.at[c, at], at_wa(w))
    ngrad = npart[w_rows(w), :].astype(f32) + nrecv[0].astype(f32)
    for k in range(1, chips):
        ngrad = ngrad + nrecv[chips + k].astype(f32)
    back = norm_backward(ngrad, gain[...].reshape(1, width), normed[...], inv[:, 0:1])
    sg[w_rows(w), :] = (cot[w_rows(w), :].astype(f32) + back).astype(bf16)
    gather_start(sg, a2_s, a2_r)
    gather_end(sg, a2_s, a2_r)

    gmask[...] = (
        lax.dot_general(sg[...], ow[...], nt, preferred_element_type=f32).astype(bf16).astype(f32)
        * own_mark
    ).astype(bf16)

    def weight_tile(cols):
        wsend[cols, :] = lax.dot_general(sg[:, cols], att[...], tn, preferred_element_type=f32).astype(bf16)


    late = (n_h - 1) * n_t

    def weight_slot(k, tt):
        return (k - 1) * n_t + tt

    def send_weight():
        for tt in range(n_t):
            for k in range(1, n_h):
                hh = lax.rem(h + k, n_h)
                at = weight_slot(k, tt)
                send(
                    wsend.at[slab_rows(tt * n_h + hh)], wrecv.at[at],
                    wg_s.at[at], wg_r.at[at], at_group(t, hh),
                )

    def height_sum(tt):
        both = wsend[slab_rows(tt * n_h + h), :].astype(f32)
        for k in range(1, n_h):
            both = both + wrecv[weight_slot(k, tt)].astype(f32)
        return both

    def relay_weight():
        for at in range(late):
            arrived(wrecv.at[at], wg_s.at[at], wg_r.at[at], at_group(t, h))
        for k in range(1, n_t):
            tt = lax.rem(t + k, n_t)
            block = slab_rows(tt * n_h + h)
            wsend[block, :] = height_sum(tt).astype(bf16)
            at = late + k - 1
            send(wsend.at[block], wrecv.at[at], wg_s.at[at], wg_r.at[at], at_group(tt, h))

    def back_head(e):
        cols = pl.ds(e * HS, HS)
        grad = gmask[:, cols]
        total[:, 0:1] = jnp.sum(grad.astype(f32) * mix[:, cols], axis=1, keepdims=True)
        mix[:, cols] = jnp.zeros((rows, HS), f32)

        def tile(slot):
            p = probs[e, slot]
            gp = lax.dot_general(gmask[:, cols], kv[slot, value_rows, cols], nt, preferred_element_type=f32)
            ds = (p.astype(f32) * (gp - total[:, 0:1]) * score_scale).astype(bf16)
            mix[:, cols] = mix[:, cols] + jnp.dot(ds, kv[slot, key_rows, cols], preferred_element_type=f32)
            psend[slot, key_rows, cols] = lax.dot_general(
                ds, q[:, cols], tn, preferred_element_type=f32
            ).astype(bf16)
            psend[slot, value_rows, cols] = lax.dot_general(
                p, gmask[:, cols], tn, preferred_element_type=f32
            ).astype(bf16)

        each_tile(tile)
        for j in (0, 2, 1):
            for i in (0, 2):
                tt, hh = t + i - 1, h + j - 1
                land = (2 - i) * 3 + j
                send(
                    psend.at[i * 3 + j, :, cols], precv.at[land, :, cols],
                    pt_s.at[e, land], pt_r.at[e, land], at_group(tt, h), inside(tt, hh),
                )

    def part_wait(e, slot):
        tt, hh = place(slot)
        block = precv.at[slot, :, pl.ds(e * HS, HS)]
        arrived(block, pt_s.at[e, slot], pt_r.at[e, slot], at_group(t, h), inside(tt, hh))

    def sum_time(e):
        cols = pl.ds(e * HS, HS)
        for j in (0, 2, 1):
            here = inside(t, h + j - 1)
            base = e * HS if j == 1 else 2 * channels
            gap = channels if j == 1 else HS
            key_acc, value_acc = pl.ds(base, HS), pl.ds(base + gap, HS)
            for i in (0, 2):
                part_wait(e, i * 3 + j)

            def begin():
                act[:, key_acc] = psend[3 + j, key_rows, cols].astype(f32)
                act[:, value_acc] = psend[3 + j, value_rows, cols].astype(f32)

            pl.when(here)(begin)
            for i in (0, 2):

                def add():
                    act[:, key_acc] = act[:, key_acc] + precv[i * 3 + j, key_rows, cols].astype(f32)
                    act[:, value_acc] = act[:, value_acc] + precv[i * 3 + j, value_rows, cols].astype(f32)

                pl.when(inside(t + i - 1, h + j - 1))(add)
            if j == 1:
                continue

            def settle():
                psend[3 + j, key_rows, cols] = act[:, key_acc].astype(bf16)
                psend[3 + j, value_rows, cols] = act[:, value_acc].astype(bf16)

            pl.when(here)(settle)
            send(
                psend.at[3 + j, :, cols], precv.at[5 - j, :, cols],
                pt_s.at[e, 5 - j], pt_r.at[e, 5 - j], at_group(t, h + j - 1), here,
            )

    for e in range(heads):
        back_head(e)
        if e == 0:
            col_tiles(width, weight_tile)
            send_weight()
    relay_weight()
    qg[...] = mix[...].astype(bf16)
    for e in range(heads):
        sum_time(e)
    wsum = height_sum(t)
    for at in range(late, late + n_t - 1):
        arrived(wrecv.at[at], wg_s.at[at], wg_r.at[at], at_group(t, h))
        wsum = wsum + wrecv[at].astype(f32)
    wg[...] = wsum
    for slot in (3, 5):
        for e in range(heads):
            part_wait(e, slot)
        tt, hh = place(slot)

        def gather(slot=slot):
            both = pl.ds(channels, channels)
            act[:, pl.ds(0, channels)] = act[:, pl.ds(0, channels)] + precv[slot, key_rows, :].astype(f32)
            act[:, both] = act[:, both] + precv[slot, value_rows, :].astype(f32)

        pl.when(inside(tt, hh))(gather)
    kg[...] = act[:, pl.ds(0, channels)].astype(bf16)
    vg[...] = act[:, pl.ds(channels, channels)].astype(bf16)
    for copy, cond in pending:
        if cond is None:
            copy.wait_send()
        else:
            pl.when(cond)(copy.wait_send)


def fused_shards(
    stream, queries, key_heads, value_heads, out_weight, norm_gain, up_weight, down_weight,
    tile_route, cotangent,
):
    n_t, n_h, n_w = (lax.axis_size(a) for a in ("ta", "ha", "wa"))
    n = n_t * n_h
    rows, width = stream.shape[2:]
    channels = queries.shape[3]
    heads = channels // HS
    slab, hidden = up_weight.shape
    share = rows // n_w
    bf16, f32 = jnp.bfloat16, jnp.float32
    vm, dma = pltpu.VMEM, pltpu.SemaphoreType.DMA
    tiles = width // 512
    sg, qg, kg, vg, wg = pl.pallas_call(
        functools.partial(step_kernel, n_t, n_h, n_w),
        out_shape=[
            jax.ShapeDtypeStruct((rows, width), bf16),
            jax.ShapeDtypeStruct((rows, channels), bf16),
            jax.ShapeDtypeStruct((rows, channels), bf16),
            jax.ShapeDtypeStruct((rows, channels), bf16),
            jax.ShapeDtypeStruct((slab, channels), f32),
        ],
        in_specs=[pl.BlockSpec(memory_space=vm)] * 2
        + [pl.BlockSpec(memory_space=pltpu.SMEM)]
        + [pl.BlockSpec(memory_space=vm)] * 7,
        out_specs=[pl.BlockSpec(memory_space=vm)] * 5,
        scratch_shapes=[
            vm((WINDOW, 2 * TILE + 16, channels), bf16),
            vm((width, hidden), bf16),
            vm((width, hidden), bf16),
            vm((WINDOW, TILE, TILE), f32),
            vm((rows, 128), f32),
            vm((rows, 128), f32),
            vm((heads, WINDOW, TILE, TILE), bf16),
            vm((rows, channels), f32),
            vm((rows, channels), bf16),
            vm((rows, width), bf16),
            vm((n_w, share, width), bf16),
            vm((rows, width), bf16),
            vm((share, width), f32),
            vm((share, 128), f32),
            vm((rows, hidden), f32),
            vm((rows, hidden), bf16),
            vm((rows, width), bf16),
            vm((n_w, share, width), bf16),
            vm((rows, channels), bf16),
            vm((width, channels), bf16),
            vm((n, slab, channels), bf16),
            vm((WINDOW, 2 * TILE, channels), bf16),
            vm((WINDOW, 2 * TILE, channels), bf16),
            dma((WINDOW,)), dma((WINDOW,)),
            dma((2, 4, n)), dma((2, n)),
            dma((n_w,)), dma((n_w,)), dma((n_w,)), dma((n_w,)),
            dma((tiles, n_w)), dma((tiles, n_w)), dma((n_w,)), dma((n_w,)),
            dma((n,)), dma((n,)),
            dma((heads, WINDOW)), dma((heads, WINDOW)),
        ],
        compiler_params=pltpu.CompilerParams(
            collective_id=0, has_side_effects=True, vmem_limit_bytes=62 * 1024 * 1024
        ),
    )(
        key_heads.reshape(rows, channels), value_heads.reshape(rows, channels), tile_route,
        queries.reshape(rows, channels), stream.reshape(rows, width),
        cotangent.reshape(rows, width), out_weight, norm_gain,
        up_weight, down_weight.T,
    )
    cell = (1, 1, rows)
    return (
        sg.reshape(cell + (width,)),
        qg.reshape(cell + (channels,)),
        kg.reshape(cell + (channels,)),
        vg.reshape(cell + (channels,)),
        wg.T,
    )


def fits_kernel(mesh, stream, up_weight, tile_route):
    n = mesh.shape["ta"] * mesh.shape["ha"]
    slab = up_weight.shape[0] // n
    share = stream.shape[2] // mesh.shape["wa"]
    pairs = mesh.shape["wa"] % 2 == 0
    return pairs and slab % 16 == 0 and share % 16 == 0 and tile_route.shape[2] == 1 and stream.shape[3] % 512 == 0


def solution(mesh):
    placed = (
        P("ta", "ha", None, None),
        P("ta", "ha", None, "wa"),
        P("ta", "ha", None, "wa"),
        P("ta", "ha", None, "wa"),
        P("wa", None),
        P(),
        P(("ta", "ha"), "wa"),
        P("wa", ("ta", "ha")),
        P("ta", "ha", None),
        P("ta", "ha", None, None),
    )
    def run(*args):
        chosen = fused_shards if fits_kernel(mesh, args[0], args[6], args[8]) else shards
        return placed_call(chosen)(*args)

    placed_call = lambda body: jax.shard_map(
        body,
        mesh=mesh,
        in_specs=placed,
        out_specs=(
            P("ta", "ha", None, None),
            P("ta", "ha", None, "wa"),
            P("ta", "ha", None, "wa"),
            P("ta", "ha", None, "wa"),
            P("wa", ("ta", "ha")),
        ),
        check_vma=False,
    )

    return run
```

```python
import functools
import math

import jax
import jax.numpy as jnp
from jax import lax
from jax.experimental import pallas as pl
from jax.experimental.pallas import tpu as pltpu
from jax.sharding import PartitionSpec as P

HS = 128
TILE = 384


EPSILON = 1e-06
TANH_SCALE = 0.7978845608028654
CUBIC_COEF = 0.044715
NEG_FILL = -1e30


def extended(cells, sides, width):
    for axis, dim in sides:
        count = lax.axis_size(axis)
        ends = count - 1
        head = lax.slice_in_dim(cells, 0, width, axis=dim)
        tail = lax.slice_in_dim(cells, cells.shape[dim] - width, cells.shape[dim], axis=dim)
        cells = jnp.concatenate(
            [
                lax.ppermute(tail, axis, [(i, (i + 1) % count) for i in range(ends)]),
                cells,
                lax.ppermute(head, axis, [((i + 1) % count, i) for i in range(ends)]),
            ],
            axis=dim,
        )
    return cells


def from_behind(array, axis, by):
    devices = lax.axis_size(axis)
    pairs = [(i, i + by) for i in range(devices) if 0 <= i + by < devices]
    return lax.ppermute(array, axis, pairs)


def gelu_slope(pre_act):
    tanh_arg = TANH_SCALE * (pre_act + CUBIC_COEF * pre_act * pre_act * pre_act)
    tanh_val = jnp.tanh(tanh_arg)
    return 0.5 * (1.0 + tanh_val) + 0.5 * pre_act * (1.0 - tanh_val * tanh_val) * TANH_SCALE * (
        1.0 + 3.0 * CUBIC_COEF * pre_act * pre_act
    )


def head_probs(query_rows, key_rows, key_marks, score_scale):
    scores = (
        jnp.einsum("qd,kd->qk", query_rows, key_rows, preferred_element_type=jnp.float32)
        * score_scale
    )
    scores = jnp.where(key_marks[None, :] > 0.5, scores, NEG_FILL)
    row_max = jnp.max(scores, axis=1)
    weights = jnp.exp(scores - row_max[:, None])
    row_total = jnp.sum(weights, axis=1)
    return (weights / row_total[:, None], row_max, row_total)


def layer_norm(residual):
    mean_val = jnp.mean(residual, axis=1, keepdims=True)
    centered = residual - mean_val
    variance = jnp.mean(centered * centered, axis=1, keepdims=True)
    inv_std = lax.rsqrt(variance + EPSILON)
    return (centered * inv_std, inv_std)


def norm_backward(norm_grad, norm_gain, normed, inv_std):
    scaled = norm_grad * norm_gain
    return (
        scaled
        - jnp.mean(scaled, axis=1, keepdims=True)
        - normed * jnp.mean(scaled * normed, axis=1, keepdims=True)
    ) * inv_std


def shards(
    stream,
    queries,
    key_heads,
    value_heads,
    out_weight,
    norm_gain,
    up_weight,
    down_weight,
    tile_route,
    cotangent,
):
    row_count = stream.shape[2]
    model_width = stream.shape[3]
    channels = queries.shape[3]
    heads_here = channels // HS
    tile_count = row_count // TILE
    score_scale = 1.0 / math.sqrt(HS)
    tile_ids = jnp.arange(tile_count, dtype=jnp.int32)
    tile_marks = tile_route.astype(jnp.bfloat16)
    faces_key, faces_value, faces_marks = (
        extended(key_heads, (("ta", 0), ("ha", 1)), 1),
        extended(value_heads, (("ta", 0), ("ha", 1)), 1),
        extended(tile_marks, (("ta", 0), ("ha", 1)), 1),
    )

    def window():
        key_block = faces_key.reshape(9 * TILE, heads_here, HS)
        value_block = faces_value.reshape(9 * TILE, heads_here, HS)
        mark_block = faces_marks.reshape(9).astype(jnp.float32)
        key_marks = jnp.repeat(mark_block, TILE)
        query_tile = queries.reshape(TILE, heads_here, HS)
        return (
            query_tile.transpose(1, 0, 2),
            key_block.transpose(1, 0, 2),
            value_block.transpose(1, 0, 2),
            key_marks,
        )

    def forward_tile(tile_index):
        own_mark = tile_marks[0, 0, tile_index]
        query_tile, key_block, value_block, key_marks = window()

        def per_head(operands):
            query_rows, key_rows, value_rows = operands
            weights, row_max, row_total = head_probs(query_rows, key_rows, key_marks, score_scale)
            mixture = jnp.dot(
                weights.astype(jnp.bfloat16), value_rows, preferred_element_type=jnp.float32
            )
            return (mixture, row_max, row_total)

        mixture, row_max, row_total = lax.map(per_head, (query_tile, key_block, value_block))
        scaled = (mixture * own_mark.astype(jnp.float32)).astype(jnp.bfloat16)
        return (scaled.transpose(1, 0, 2).reshape(TILE, channels), row_max, row_total)

    attn_tiles, max_tiles, total_tiles = lax.map(forward_tile, tile_ids)
    attention = attn_tiles.reshape(row_count, channels)
    attn_part = jnp.dot(attention, out_weight, preferred_element_type=jnp.float32)
    head_share = lax.psum_scatter(attn_part, "wa", scatter_dimension=0, tiled=True)
    share_rows = head_share.shape[0]
    share_start = lax.axis_index("wa") * share_rows
    flat_stream = stream.reshape(row_count, model_width)
    flat_cot = cotangent.reshape(row_count, model_width)
    residual = (
        lax.dynamic_slice_in_dim(flat_stream, share_start, share_rows, 0).astype(jnp.float32)
        + head_share
    )
    normed, inv_std = layer_norm(residual)
    hidden_share = (normed * norm_gain).astype(jnp.bfloat16)
    hidden_in = lax.all_gather(hidden_share, "wa", axis=0, tiled=True)
    up_full, down_full = (
        lax.all_gather(up_weight, ("ta", "ha"), axis=0, tiled=True),
        lax.all_gather(down_weight, ("ta", "ha"), axis=1, tiled=True),
    )
    pre_act = jnp.dot(hidden_in, up_full, preferred_element_type=jnp.float32)
    act_grad = jnp.einsum("td,fd->tf", flat_cot, down_full, preferred_element_type=jnp.float32)
    pre_grad = (act_grad * gelu_slope(pre_act)).astype(jnp.bfloat16)
    norm_part = jnp.einsum("tf,df->td", pre_grad, up_full, preferred_element_type=jnp.float32)
    norm_share = lax.psum_scatter(norm_part, "wa", scatter_dimension=0, tiled=True)
    cot_share = lax.dynamic_slice_in_dim(flat_cot, share_start, share_rows, 0).astype(jnp.float32)
    grad_share = (cot_share + norm_backward(norm_share, norm_gain, normed, inv_std)).astype(
        jnp.bfloat16
    )
    stream_grad = lax.all_gather(grad_share, "wa", axis=0, tiled=True)
    weight_part = jnp.einsum(
        "tc,td->cd", attention, stream_grad, preferred_element_type=jnp.float32
    )
    out_weight_grad = lax.psum_scatter(weight_part, ("ta", "ha"), scatter_dimension=1, tiled=True)
    attn_grad = jnp.einsum(
        "td,cd->tc", stream_grad, out_weight, preferred_element_type=jnp.float32
    ).astype(jnp.bfloat16)
    row_marks = jnp.repeat(tile_marks.reshape(tile_count), TILE)
    masked_grad = attn_grad * row_marks[:, None]

    def own_side():
        query_tile, key_block, value_block, key_marks = window()
        grad_tile = masked_grad.reshape(TILE, heads_here, HS).transpose(1, 0, 2)

        def head_back(operands):
            query_rows, key_rows, value_rows, grad_rows = operands
            weights = head_probs(query_rows, key_rows, key_marks, score_scale)[0]
            grad_probs = jnp.einsum(
                "qd,kd->qk", grad_rows, value_rows, preferred_element_type=jnp.float32
            )
            row_delta = jnp.sum(weights * grad_probs, axis=1)
            grad_scores = (weights * (grad_probs - row_delta[:, None]) * score_scale).astype(
                jnp.bfloat16
            )
            query_part = jnp.dot(grad_scores, key_rows, preferred_element_type=jnp.float32).astype(
                jnp.bfloat16
            )
            value_part = jnp.einsum(
                "qk,qd->kd",
                weights.astype(jnp.bfloat16),
                grad_rows,
                preferred_element_type=jnp.float32,
            ).astype(jnp.bfloat16)
            key_part = jnp.einsum(
                "qk,qd->kd", grad_scores, query_rows, preferred_element_type=jnp.float32
            ).astype(jnp.bfloat16)
            return (query_part, row_delta, key_part, value_part)

        results = lax.map(head_back, (query_tile, key_block, value_block, grad_tile))
        query_part = results[0].transpose(1, 0, 2).reshape(TILE, channels)
        key_part = results[2].transpose(1, 0, 2).reshape(3, 3, TILE, channels)
        value_part = results[3].transpose(1, 0, 2).reshape(3, 3, TILE, channels)
        return (query_part, results[1], key_part, value_part)

    def guarded_own():
        blank_parts = (
            jnp.zeros((TILE, channels), jnp.bfloat16),
            jnp.zeros((heads_here, TILE), jnp.float32),
        )
        blank_parts = blank_parts + (
            jnp.zeros((3, 3, TILE, channels), jnp.bfloat16),
            jnp.zeros((3, 3, TILE, channels), jnp.bfloat16),
        )
        return own_side()

    def place_tile(carried, tile_index):
        query_part, row_delta, key_part, value_part = guarded_own()
        return ((key_part, value_part), query_part)

    empty_slots = jnp.zeros((3, 3, row_count, channels), jnp.bfloat16)
    (slots_key, slots_value), query_parts = lax.scan(
        place_tile, (empty_slots, empty_slots), tile_ids
    )
    middle_key = slots_key[1].astype(jnp.float32)
    middle_value = slots_value[1].astype(jnp.float32)
    for by_step, source in ((-1, 0), (1, 2)):
        moved_key, moved_value = from_behind(
            (slots_key[source], slots_value[source]), "ta", by_step
        )
        middle_key = middle_key + moved_key.astype(jnp.float32)
        middle_value = middle_value + moved_value.astype(jnp.float32)
    final_key = middle_key[1]
    final_value = middle_value[1]
    for by_step, source in ((-1, 0), (1, 2)):
        moved_key, moved_value = (
            from_behind(middle_key[source].astype(jnp.bfloat16), "ha", by_step).astype(jnp.float32),
            from_behind(middle_value[source].astype(jnp.bfloat16), "ha", by_step).astype(
                jnp.float32
            ),
        )
        final_key = final_key + moved_key
        final_value = final_value + moved_value
    key_grad = final_key.astype(jnp.bfloat16).reshape(1, 1, row_count, channels)
    value_grad = final_value.astype(jnp.bfloat16).reshape(1, 1, row_count, channels)
    query_grad = query_parts.reshape(1, 1, row_count, channels)
    return (
        stream_grad.reshape(1, 1, row_count, model_width),
        query_grad,
        key_grad,
        value_grad,
        out_weight_grad,
    )


MESH = pl.DeviceIdType.MESH
WINDOW = 9
CENTRE = 4


def step_kernel(
    n_t, n_h, n_w, keys, values, route, q, stream, cot, ow, gain, upw, dnw,
    sg, qg, kg, vg, wg,
    kv, up, dn, score, top, total, probs, mix, att, apart, arecv, hid, normed, inv,
    act, pgrad, npart, nrecv, gmask, wsend, wrecv, psend, precv,
    halo_s, halo_r, wt_s, wt_r, r1_s, r1_r, a1_s, a1_r, r2_s, r2_r, a2_s, a2_r,
    wg_s, wg_r, pt_s, pt_r,
):
    f32, bf16 = jnp.float32, jnp.bfloat16
    t, h, w = lax.axis_index("ta"), lax.axis_index("ha"), lax.axis_index("wa")
    n = n_t * n_h
    g = t * n_h + h
    rows, width = stream.shape
    channels = q.shape[1]
    heads = channels // HS
    slab = upw.shape[0]
    share = rows // n_w
    hidden = upw.shape[1]
    score_scale = 1.0 / math.sqrt(HS)
    pending = []

    def at_group(tt, hh):
        return {"ta": tt, "ha": hh}

    def at_wa(ww):
        return {"wa": ww}

    def group_peer(k):
        idx = lax.rem(g + k, n)
        return idx, at_group(idx // n_h, lax.rem(idx, n_h))

    def send(src, dst, s_sem, r_sem, dev, cond=None):
        copy = pltpu.make_async_remote_copy(
            src_ref=src, dst_ref=dst, send_sem=s_sem, recv_sem=r_sem,
            device_id=dev, device_id_type=MESH,
        )
        if cond is None:
            copy.start()
        else:
            pl.when(cond)(copy.start)
        pending.append((copy, cond))

    def arrived(dst, s_sem, r_sem, dev, cond=None):
        copy = pltpu.make_async_remote_copy(
            src_ref=dst, dst_ref=dst, send_sem=s_sem, recv_sem=r_sem,
            device_id=dev, device_id_type=MESH,
        )
        if cond is None:
            copy.wait_recv()
        else:
            pl.when(cond)(copy.wait_recv)

    def inside(tt, hh):
        return (tt >= 0) & (tt < n_t) & (hh >= 0) & (hh < n_h)

    def place(slot):
        return t + slot // 3 - 1, h + slot % 3 - 1

    def w_rows(ww):
        return pl.ds(pl.multiple_of(ww * share, share), share)

    def slab_rows(idx):
        return pl.ds(pl.multiple_of(idx * slab, slab), slab)

    pair = w + 1 - 2 * lax.rem(w, 2)
    chips = n_w // 2

    def gather_start(buf, s_sem, r_sem):
        for k in range(1, chips):
            ww = lax.rem(w + 2 * k, n_w)
            send(buf.at[w_rows(w)], buf.at[w_rows(w)], s_sem.at[k], r_sem.at[k], at_wa(ww))
        send(buf.at[w_rows(w)], buf.at[w_rows(w)], s_sem.at[0], r_sem.at[0], at_wa(pair))

    def gather_end(buf, s_sem, r_sem):
        for k in range(1, chips):
            block = buf.at[w_rows(lax.rem(w + n_w - 2 * k, n_w))]
            arrived(block, s_sem.at[k], r_sem.at[k], at_wa(w))
            send(block, block, s_sem.at[chips + k], r_sem.at[chips + k], at_wa(pair))
        arrived(buf.at[w_rows(pair)], s_sem.at[0], r_sem.at[0], at_wa(w))
        for k in range(1, chips):
            block = buf.at[w_rows(lax.rem(pair + n_w - 2 * k, n_w))]
            arrived(block, s_sem.at[chips + k], r_sem.at[chips + k], at_wa(w))

    kvm = kv.at[CENTRE]
    kv[CENTRE, pl.ds(0, TILE), :] = keys[...]
    kv[CENTRE, pl.ds(TILE, TILE), :] = values[...]
    own = jnp.full((16, channels), route[0, 0, 0], jnp.int32).astype(f32)
    kv[CENTRE, pl.ds(2 * TILE, 16), :] = own.astype(bf16)
    barrier = pltpu.get_barrier_semaphore()
    for k in range(1, n):
        pl.semaphore_signal(barrier, inc=1, device_id=group_peer(k)[1], device_id_type=MESH)
    for k in range(1, n_w):
        pl.semaphore_signal(barrier, inc=1, device_id=at_wa(lax.rem(w + k, n_w)), device_id_type=MESH)
    pl.semaphore_wait(barrier, n - 1 + n_w - 1)

    def window_send(src, slot, tt, hh, cond):
        send(src, kv.at[slot], halo_s.at[slot], halo_r.at[slot], at_group(tt, hh), cond)

    def window_wait(slot):
        tt, hh = place(slot)
        arrived(kv.at[slot], halo_s.at[slot], halo_r.at[slot], at_group(t, h), inside(tt, hh))

    window_send(kvm, 3, t, h + 1, inside(t, h + 1))
    window_send(kvm, 5, t, h - 1, inside(t, h - 1))

    weights = (dn, up)

    def hop(which, src_ref, idx, way):
        tt, hh = ((t + 1, h), (t - 1, h), (t, h + 1), (t, h - 1))[way]
        return (
            src_ref, weights[which].at[slab_rows(idx)], wt_s.at[which, way, idx],
            wt_r.at[which, idx], at_group(tt, hh),
        ), inside(tt, hh)

    def forward(which, src_ref, idx, ways, cond=None):
        for way in ways:
            args, here = hop(which, src_ref, idx, way)
            send(*args, here if cond is None else here & cond)

    forward(0, dnw, g, (0, 1, 2, 3))
    window_send(kvm, 1, t + 1, h, inside(t + 1, h))
    window_send(kvm, 7, t - 1, h, inside(t - 1, h))
    forward(1, upw, g, (2, 3))

    def relay(which, d):
        for sign, way in ((1, 0), (-1, 1)):
            tt = t - sign * d
            cond = inside(tt, h)
            idx = jnp.clip(tt, 0, n_t - 1) * n_h + h
            block = weights[which].at[slab_rows(idx)]
            arrived(block, wt_s.at[which, way, idx], wt_r.at[which, idx], at_group(t, h), cond)
            forward(which, block, idx, (2, 3, way), cond)

    def finish(which):
        for e in range(1, n_h):
            for sign, way in ((1, 2), (-1, 3)):
                hh = h - sign * e
                for d in range(-(n_t - 1), n_t):
                    tt = t + d
                    cond = inside(tt, hh)
                    idx = jnp.clip(tt, 0, n_t - 1) * n_h + jnp.clip(hh, 0, n_h - 1)
                    block = weights[which].at[slab_rows(idx)]
                    arrived(block, wt_s.at[which, way, idx], wt_r.at[which, idx], at_group(t, h), cond)
                    if e < n_h - 1:
                        forward(which, block, idx, (way,), cond)

    dn[slab_rows(g), :] = dnw[...]
    up[slab_rows(g), :] = upw[...]

    for j in (0, 2):
        window_wait(3 + j)
        here = inside(t, h + j - 1)
        window_send(kv.at[3 + j], j, t + 1, h, inside(t + 1, h) & here)
        window_send(kv.at[3 + j], 6 + j, t - 1, h, inside(t - 1, h) & here)
    forward(1, upw, g, (0, 1))
    relay(0, 1)
    for slot in (1, 7, 0, 2, 6, 8):
        window_wait(slot)

    def each_tile(work):
        @pl.loop(0, WINDOW)
        def _(slot):
            tt, hh = place(slot)
            pl.when(inside(tt, hh))(lambda: work(slot))

    nt = (((1,), (1,)), ((), ()))
    tn = (((0,), (0,)), ((), ()))
    key_rows, value_rows = pl.ds(0, TILE), pl.ds(TILE, TILE)
    own_mark = kv[CENTRE, pl.ds(2 * TILE, 1), :].astype(f32)

    def attend(e):
        cols = pl.ds(e * HS, HS)
        top[...] = jnp.full(top.shape, NEG_FILL, f32)
        total[...] = jnp.zeros(total.shape, f32)
        mix[:, cols] = jnp.zeros((rows, HS), f32)

        def raw(slot):
            s = lax.dot_general(q[:, cols], kv[slot, key_rows, cols], nt, preferred_element_type=f32)
            mark = kv[slot, pl.ds(2 * TILE, 1), :].astype(f32)
            s = jnp.where(mark > 0.5, s * score_scale, NEG_FILL)
            score[slot] = s
            top[...] = jnp.maximum(top[...], jnp.max(s, axis=1, keepdims=True))

        each_tile(raw)

        def expo(slot):
            p = jnp.exp(score[slot] - top[:, 0:1])
            score[slot] = p
            total[...] = total[...] + jnp.sum(p, axis=1, keepdims=True)

        each_tile(expo)
        total[...] = 1.0 / total[...]

        def blend(slot):
            p = (score[slot] * total[:, 0:1]).astype(bf16)
            probs[e, slot] = p
            mix[:, cols] = mix[:, cols] + jnp.dot(p, kv[slot, value_rows, cols], preferred_element_type=f32)

        each_tile(blend)

    for e in range(heads):
        attend(e)
        if e == 0:
            relay(1, 1)
    if n_t > 2:
        relay(0, 2)
    att[...] = (mix[...] * own_mark).astype(bf16)
    step = 512

    def col_tiles(count, work):
        @pl.loop(0, count // step)
        def _(c):
            work(pl.ds(pl.multiple_of(c * step, step), step))

    def project(cols):
        apart[:, cols] = jnp.dot(att[...], ow[:, cols], preferred_element_type=f32).astype(bf16)

    col_tiles(width, project)
    for k in range(1, n_w):
        ww = lax.rem(w + k, n_w)
        send(apart.at[w_rows(ww)], arecv.at[k], r1_s.at[k], r1_r.at[k], at_wa(ww))
    resid = stream[w_rows(w), :].astype(f32) + apart[w_rows(w), :].astype(f32)
    for k in range(1, n_w):
        arrived(arecv.at[k], r1_s.at[k], r1_r.at[k], at_wa(w))
        resid = resid + arecv[k].astype(f32)
    centered = resid - jnp.mean(resid, axis=1, keepdims=True)
    istd = lax.rsqrt(jnp.mean(centered * centered, axis=1, keepdims=True) + EPSILON)
    inv[...] = jnp.broadcast_to(istd, inv.shape)
    normed[...] = centered * istd
    hid[w_rows(w), :] = (normed[...] * gain[...].reshape(1, width)).astype(bf16)
    gather_start(hid, a1_s, a1_r)
    for d in range(2, n_t):
        if d > 2:
            relay(0, d)
        relay(1, d)
    finish(0)

    def act_tile(cols):
        act[:, cols] = jnp.dot(cot[...], dn[:, cols], preferred_element_type=f32)

    col_tiles(hidden, act_tile)
    gather_end(hid, a1_s, a1_r)
    finish(1)

    def grad_tile(cols):
        pre = jnp.dot(hid[...], up[:, cols], preferred_element_type=f32)
        pgrad[:, cols] = (act[:, cols] * gelu_slope(pre)).astype(bf16)

    col_tiles(hidden, grad_tile)
    def pair_sums(c):
        cols = pl.ds(c * step, step)
        for k in range(chips - 1, -1, -1):
            block = nrecv.at[k, :, cols]
            arrived(block, r2_s.at[c, k], r2_r.at[c, k], at_wa(w))
            if k == 0:
                continue
            ww = lax.rem(w + 2 * k, n_w)
            both = npart[w_rows(ww), cols].astype(f32) + nrecv[k, :, cols].astype(f32)
            npart[w_rows(ww), cols] = both.astype(bf16)
            send(
                npart.at[w_rows(ww), cols], nrecv.at[chips + k, :, cols],
                r2_s.at[c, chips + k], r2_r.at[c, chips + k], at_wa(ww),
            )

    for c in range(width // step):
        cols = pl.ds(c * step, step)
        npart[:, cols] = lax.dot_general(
            pgrad[...], up[cols, :], nt, preferred_element_type=f32
        ).astype(bf16)
        for k in range(chips - 1, -1, -1):
            ww = lax.rem(pair + 2 * k, n_w)
            send(
                npart.at[w_rows(ww), cols], nrecv.at[k, :, cols],
                r2_s.at[c, k], r2_r.at[c, k], at_wa(pair),
            )
        if c >= 1:
            pair_sums(c - 1)
    pair_sums(width // step - 1)
    for k in range(1, chips):
        for c in range(width // step):
            at = chips + k
            arrived(nrecv.at[at, :, pl.ds(c * step, step)], r2_s.at[c, at], r2_r.at[c, at], at_wa(w))
    ngrad = npart[w_rows(w), :].astype(f32) + nrecv[0].astype(f32)
    for k in range(1, chips):
        ngrad = ngrad + nrecv[chips + k].astype(f32)
    back = norm_backward(ngrad, gain[...].reshape(1, width), normed[...], inv[:, 0:1])
    sg[w_rows(w), :] = (cot[w_rows(w), :].astype(f32) + back).astype(bf16)
    gather_start(sg, a2_s, a2_r)
    gather_end(sg, a2_s, a2_r)

    gmask[...] = (
        lax.dot_general(sg[...], ow[...], nt, preferred_element_type=f32).astype(bf16).astype(f32)
        * own_mark
    ).astype(bf16)

    def weight_tile(cols):
        wsend[cols, :] = lax.dot_general(sg[:, cols], att[...], tn, preferred_element_type=f32).astype(bf16)


    late = (n_h - 1) * n_t

    def weight_slot(k, tt):
        return (k - 1) * n_t + tt

    def send_weight():
        for tt in range(n_t):
            for k in range(1, n_h):
                hh = lax.rem(h + k, n_h)
                at = weight_slot(k, tt)
                send(
                    wsend.at[slab_rows(tt * n_h + hh)], wrecv.at[at],
                    wg_s.at[at], wg_r.at[at], at_group(t, hh),
                )

    def height_sum(tt):
        both = wsend[slab_rows(tt * n_h + h), :].astype(f32)
        for k in range(1, n_h):
            both = both + wrecv[weight_slot(k, tt)].astype(f32)
        return both

    def relay_weight():
        for at in range(late):
            arrived(wrecv.at[at], wg_s.at[at], wg_r.at[at], at_group(t, h))
        for k in range(1, n_t):
            tt = lax.rem(t + k, n_t)
            block = slab_rows(tt * n_h + h)
            wsend[block, :] = height_sum(tt).astype(bf16)
            at = late + k - 1
            send(wsend.at[block], wrecv.at[at], wg_s.at[at], wg_r.at[at], at_group(tt, h))

    def back_head(e):
        cols = pl.ds(e * HS, HS)
        grad = gmask[:, cols]
        total[:, 0:1] = jnp.sum(grad.astype(f32) * mix[:, cols], axis=1, keepdims=True)
        mix[:, cols] = jnp.zeros((rows, HS), f32)

        def tile(slot):
            p = probs[e, slot]
            gp = lax.dot_general(gmask[:, cols], kv[slot, value_rows, cols], nt, preferred_element_type=f32)
            ds = (p.astype(f32) * (gp - total[:, 0:1]) * score_scale).astype(bf16)
            mix[:, cols] = mix[:, cols] + jnp.dot(ds, kv[slot, key_rows, cols], preferred_element_type=f32)
            psend[slot, key_rows, cols] = lax.dot_general(
                ds, q[:, cols], tn, preferred_element_type=f32
            ).astype(bf16)
            psend[slot, value_rows, cols] = lax.dot_general(
                p, gmask[:, cols], tn, preferred_element_type=f32
            ).astype(bf16)

        each_tile(tile)
        for j in (0, 2, 1):
            for i in (0, 2):
                tt, hh = t + i - 1, h + j - 1
                land = (2 - i) * 3 + j
                send(
                    psend.at[i * 3 + j, :, cols], precv.at[land, :, cols],
                    pt_s.at[e, land], pt_r.at[e, land], at_group(tt, h), inside(tt, hh),
                )

    def part_wait(e, slot):
        tt, hh = place(slot)
        block = precv.at[slot, :, pl.ds(e * HS, HS)]
        arrived(block, pt_s.at[e, slot], pt_r.at[e, slot], at_group(t, h), inside(tt, hh))

    def sum_time(e):
        cols = pl.ds(e * HS, HS)
        for j in (0, 2, 1):
            here = inside(t, h + j - 1)
            base = e * HS if j == 1 else 2 * channels
            gap = channels if j == 1 else HS
            key_acc, value_acc = pl.ds(base, HS), pl.ds(base + gap, HS)
            for i in (0, 2):
                part_wait(e, i * 3 + j)

            def begin():
                act[:, key_acc] = psend[3 + j, key_rows, cols].astype(f32)
                act[:, value_acc] = psend[3 + j, value_rows, cols].astype(f32)

            pl.when(here)(begin)
            for i in (0, 2):

                def add():
                    act[:, key_acc] = act[:, key_acc] + precv[i * 3 + j, key_rows, cols].astype(f32)
                    act[:, value_acc] = act[:, value_acc] + precv[i * 3 + j, value_rows, cols].astype(f32)

                pl.when(inside(t + i - 1, h + j - 1))(add)
            if j == 1:
                continue

            def settle():
                psend[3 + j, key_rows, cols] = act[:, key_acc].astype(bf16)
                psend[3 + j, value_rows, cols] = act[:, value_acc].astype(bf16)

            pl.when(here)(settle)
            send(
                psend.at[3 + j, :, cols], precv.at[5 - j, :, cols],
                pt_s.at[e, 5 - j], pt_r.at[e, 5 - j], at_group(t, h + j - 1), here,
            )

    for e in range(heads):
        back_head(e)
        if e == 0:
            col_tiles(width, weight_tile)
            send_weight()
    relay_weight()
    qg[...] = mix[...].astype(bf16)
    for e in range(heads):
        sum_time(e)
    wsum = height_sum(t)
    for at in range(late, late + n_t - 1):
        arrived(wrecv.at[at], wg_s.at[at], wg_r.at[at], at_group(t, h))
        wsum = wsum + wrecv[at].astype(f32)
    wg[...] = wsum
    for slot in (3, 5):
        for e in range(heads):
            part_wait(e, slot)
        tt, hh = place(slot)

        def gather(slot=slot):
            both = pl.ds(channels, channels)
            act[:, pl.ds(0, channels)] = act[:, pl.ds(0, channels)] + precv[slot, key_rows, :].astype(f32)
            act[:, both] = act[:, both] + precv[slot, value_rows, :].astype(f32)

        pl.when(inside(tt, hh))(gather)
    kg[...] = act[:, pl.ds(0, channels)].astype(bf16)
    vg[...] = act[:, pl.ds(channels, channels)].astype(bf16)
    for copy, cond in pending:
        if cond is None:
            copy.wait_send()
        else:
            pl.when(cond)(copy.wait_send)


def fused_shards(
    stream, queries, key_heads, value_heads, out_weight, norm_gain, up_weight, down_weight,
    tile_route, cotangent,
):
    n_t, n_h, n_w = (lax.axis_size(a) for a in ("ta", "ha", "wa"))
    n = n_t * n_h
    rows, width = stream.shape[2:]
    channels = queries.shape[3]
    heads = channels // HS
    slab, hidden = up_weight.shape
    share = rows // n_w
    bf16, f32 = jnp.bfloat16, jnp.float32
    vm, dma = pltpu.VMEM, pltpu.SemaphoreType.DMA
    tiles = width // 512
    sg, qg, kg, vg, wg = pl.pallas_call(
        functools.partial(step_kernel, n_t, n_h, n_w),
        out_shape=[
            jax.ShapeDtypeStruct((rows, width), bf16),
            jax.ShapeDtypeStruct((rows, channels), bf16),
            jax.ShapeDtypeStruct((rows, channels), bf16),
            jax.ShapeDtypeStruct((rows, channels), bf16),
            jax.ShapeDtypeStruct((slab, channels), f32),
        ],
        in_specs=[pl.BlockSpec(memory_space=vm)] * 2
        + [pl.BlockSpec(memory_space=pltpu.SMEM)]
        + [pl.BlockSpec(memory_space=vm)] * 7,
        out_specs=[pl.BlockSpec(memory_space=vm)] * 5,
        scratch_shapes=[
            vm((WINDOW, 2 * TILE + 16, channels), bf16),
            vm((width, hidden), bf16),
            vm((width, hidden), bf16),
            vm((WINDOW, TILE, TILE), f32),
            vm((rows, 128), f32),
            vm((rows, 128), f32),
            vm((heads, WINDOW, TILE, TILE), bf16),
            vm((rows, channels), f32),
            vm((rows, channels), bf16),
            vm((rows, width), bf16),
            vm((n_w, share, width), bf16),
            vm((rows, width), bf16),
            vm((share, width), f32),
            vm((share, 128), f32),
            vm((rows, hidden), f32),
            vm((rows, hidden), bf16),
            vm((rows, width), bf16),
            vm((n_w, share, width), bf16),
            vm((rows, channels), bf16),
            vm((width, channels), bf16),
            vm((n, slab, channels), bf16),
            vm((WINDOW, 2 * TILE, channels), bf16),
            vm((WINDOW, 2 * TILE, channels), bf16),
            dma((WINDOW,)), dma((WINDOW,)),
            dma((2, 4, n)), dma((2, n)),
            dma((n_w,)), dma((n_w,)), dma((n_w,)), dma((n_w,)),
            dma((tiles, n_w)), dma((tiles, n_w)), dma((n_w,)), dma((n_w,)),
            dma((n,)), dma((n,)),
            dma((heads, WINDOW)), dma((heads, WINDOW)),
        ],
        compiler_params=pltpu.CompilerParams(
            collective_id=0, has_side_effects=True, vmem_limit_bytes=62 * 1024 * 1024
        ),
    )(
        key_heads.reshape(rows, channels), value_heads.reshape(rows, channels), tile_route,
        queries.reshape(rows, channels), stream.reshape(rows, width),
        cotangent.reshape(rows, width), out_weight, norm_gain,
        up_weight, down_weight.T,
    )
    cell = (1, 1, rows)
    return (
        sg.reshape(cell + (width,)),
        qg.reshape(cell + (channels,)),
        kg.reshape(cell + (channels,)),
        vg.reshape(cell + (channels,)),
        wg.T,
    )


def fits_kernel(mesh, stream, up_weight, tile_route):
    n = mesh.shape["ta"] * mesh.shape["ha"]
    slab = up_weight.shape[0] // n
    share = stream.shape[2] // mesh.shape["wa"]
    pairs = mesh.shape["wa"] % 2 == 0
    return pairs and slab % 16 == 0 and share % 16 == 0 and tile_route.shape[2] == 1 and stream.shape[3] % 512 == 0


def solution(mesh):
    placed = (
        P("ta", "ha", None, None),
        P("ta", "ha", None, "wa"),
        P("ta", "ha", None, "wa"),
        P("ta", "ha", None, "wa"),
        P("wa", None),
        P(),
        P(("ta", "ha"), "wa"),
        P("wa", ("ta", "ha")),
        P("ta", "ha", None),
        P("ta", "ha", None, None),
    )
    def run(*args):
        chosen = fused_shards if fits_kernel(mesh, args[0], args[6], args[8]) else shards
        return placed_call(chosen)(*args)

    placed_call = lambda body: jax.shard_map(
        body,
        mesh=mesh,
        in_specs=placed,
        out_specs=(
            P("ta", "ha", None, None),
            P("ta", "ha", None, "wa"),
            P("ta", "ha", None, "wa"),
            P("ta", "ha", None, "wa"),
            P("wa", ("ta", "ha")),
        ),
        check_vma=False,
    )

    return run
```
